768 devices in a mesh: dp: 16 (over y, core), fsdp: 48 (over z, x).
Axes of the slice: x: 4, y: 8, z: 12, core: 2. Of those that a mesh axis runs over, the one named last changes fastest.
Arguments:
- x_slots: bfloat16 [48, 3072, 4608], P('fsdp', None, 'dp'), may hold values from -6 to 6
- gain: bfloat16 [4608], P('fsdp'), may hold values from 0.099609375 to 1.8984375
- adapter: bfloat16 [4608, 256], P('fsdp'), may hold values from -0.09375 to 0.09375
- readout: bfloat16 [48, 3072, 256], P('fsdp'), may hold values from -0.1875 to 0.1875
- drift: float32 [48, 3072], P('fsdp'), may hold values from -0.6 to 0.6
- ref_gap: float32 [48, 3072], P('fsdp'), may hold values from -2 to 2
- rewards: float32 [48, 48], P('fsdp'), may hold values from -4 to 4
- groups: int32 [48, 48], P('fsdp'), may hold values from 0 to 11, never falling along the last dimension, each value on 1 to 8 neighbouring positions
- lengths: int32 [48, 48], P('fsdp'), may hold values from 1 to 64, as said below
- dest: int32 [48, 48], P('fsdp'), may hold values from 0 to 15, as said below
Outputs:
- grad_adapter: float32 [4608, 256], P('fsdp')
- grad_gain: float32 [4608], P('fsdp')
The draws below stay inside these ranges and needn't reach their ends.
Inputs may be any that keep to these rules, and one draw needn't show every extreme that they name: `dest`: each learner rank receives exactly 3 rollouts of every column. `lengths`: in every column, all rollouts of some learner rank have 64 tokens, so that some rank holds exactly 192 live tokens. `groups`: within a column group numbers never fall; a group has 1 to 8 rollouts.
All inputs are finite; a program needn't handle non-finite values.
Results may differ from the reference program's by a relative error of at most 0.0045.
Values may be sent and summed in bfloat16 or wider, within the bound.
A program may use at most 64 MiB of HBM per device.

```python
import math
import jax
import jax.numpy as jnp
import numpy as np
from jax import lax

D = 4608
R = 256
LMAX = 64
ROLL_RANK = 3
GROUP_MOST = 8
ROLL_COL = 48
SLOTS = 3072
GROUPS = 12
N_DP = 16
N_FSDP = 48


def shared_layout(key):
    column_keys = jax.random.split(key, N_FSDP)

    def one_column(column_key):
        perm_key, len_key, full_key = jax.random.split(column_key, 3)
        order_perm = jax.random.permutation(perm_key, ROLL_COL)
        targets = (order_perm // ROLL_RANK).astype(jnp.int32)
        roll_lengths = jax.random.randint(len_key, (ROLL_COL,), 1, LMAX + 1)
        full_rank = jax.random.randint(full_key, (), 0, ROLL_COL // ROLL_RANK)
        roll_lengths = jnp.where(targets == full_rank, LMAX, roll_lengths)
        return (roll_lengths.astype(jnp.int32), targets)
    return jax.vmap(one_column)(column_keys)


def draw_lengths(key, part):
    roll_lengths, targets = shared_layout(key)
    return roll_lengths


def draw_dest(key, part):
    roll_lengths, targets = shared_layout(key)
    return targets


def raised(values, own_key, source, target, parts, factor):
    def block_of(dim):
        return (jnp.arange(values.shape[dim]) // (values.shape[dim] // parts)).reshape((-1,) + (1,) * (values.ndim - 1 - dim))

    one_side = jax.random.permutation(own_key, parts)[block_of(target)]
    other_side = (block_of(target) + parts // 2) % parts
    return jnp.where((block_of(source) == one_side) | (block_of(source) == other_side), factor * values, values)


def steps_of(rng, extent, shards, low, largest):
    loudness = 1.0
    for dim, shards_of in shards:
        draws = jax.random.uniform(jax.random.fold_in(jax.random.fold_in(rng, 6), dim), (shards_of,), jnp.float32, low / len(shards), largest / len(shards))
        loudness = loudness * jnp.repeat(jnp.exp(draws), extent[dim] // shards_of).reshape((-1,) + (1,) * (len(extent) - 1 - dim))
    return loudness


def profile(number_of, total, most, lean):
    loads = [(1 << 20) // math.isqrt(standing ** lean) + 1 for standing in range(2, number_of + 1)]
    rest, counts = total - most - (number_of - 1), [1] * (number_of - 1)
    while rest > 0:
        candidates = [i for i in range(number_of - 1) if counts[i] < most]
        whole, budget = sum([loads[i] for i in candidates]), rest
        for i in candidates:
            addition = min(most - counts[i], max(1, budget * loads[i] // whole), rest)
            counts[i] = counts[i] + addition
            rest = rest - addition
    return np.array([most] + counts)


def uneven(own_key, number_of, total, reach, skew):
    if number_of == 2:
        one = jax.random.randint(own_key, (), max(1, total - reach), min(reach, total - 1) + 1)
        return jnp.stack([one, total - one])
    sizes = jnp.asarray(profile(number_of, total, reach, skew), jnp.int32)
    couples = (number_of - 1) // 2
    giver, sink = sizes[1:1 + 2 * couples:2], sizes[2:2 + 2 * couples:2]
    margin = jnp.minimum(giver - 1, reach - sink)
    passed = jax.random.randint(jax.random.fold_in(own_key, 1), (couples,), 0, 1 << 20) % (margin + 1)
    sizes = sizes.at[1:1 + 2 * couples:2].set(giver - passed).at[2:2 + 2 * couples:2].set(sink + passed)
    return sizes[jax.random.permutation(jax.random.fold_in(own_key, 2), number_of)]


def gaussian(key, shape, width, bound, pieces=(), kind=jnp.bfloat16):
    entries = jax.random.normal(key, shape, jnp.float32) * width
    if len(pieces) > 0:
        entries = steps_of(key, shape, pieces, -0.22, 0.18) * entries
    return jnp.clip(entries, min=-bound, max=bound).astype(kind)


def noise_with(stream_key, dims, deviation, most, cuts, heavy, kind=jnp.bfloat16):
    drawn = deviation * jax.random.normal(stream_key, dims, jnp.float32)
    if cuts:
        drawn = drawn * steps_of(stream_key, dims, cuts, -0.22, 0.18)
    return jnp.clip(raised(drawn, jax.random.fold_in(stream_key, 3), *heavy), -most, most).astype(kind)


def setup_inputs(seed: int = 0) -> dict:
    arg_keys = jax.random.split(jax.random.key(seed), 11)
    x_slots = noise_with(arg_keys[0], (N_FSDP, SLOTS, D), 1.0, 6.0, ((0, 48), (2, 16)), (0, 2, 48, 3.25))
    gain = jnp.clip(1.0 + 0.18 * jax.random.normal(arg_keys[1], (D,), jnp.float32), 0.099609375, 1.8984375).astype(jnp.bfloat16)
    adapter = gaussian(arg_keys[2], (D, R), D ** -0.5, 0.09375, ((0, 48),))
    readout = gaussian(arg_keys[3], (N_FSDP, SLOTS, R), (4 * R) ** -0.5, 0.1875, ((0, 48),))
    drift = gaussian(arg_keys[4], (N_FSDP, SLOTS), 0.15, 0.6, ((0, 48),), jnp.float32)
    ref_gap = gaussian(arg_keys[5], (N_FSDP, SLOTS), 0.5, 2.0, ((0, 48),), jnp.float32)
    rewards = gaussian(arg_keys[6], (N_FSDP, ROLL_COL), 1.0, 4.0, ((0, 48),), jnp.float32)
    groups = jax.vmap(lambda own: jnp.searchsorted(jnp.cumsum(uneven(own, GROUPS, ROLL_COL, GROUP_MOST, 1)), jnp.arange(ROLL_COL), side="right"))(jax.random.split(arg_keys[7], N_FSDP)).reshape((N_FSDP, ROLL_COL)).astype(jnp.int32)
    lengths = draw_lengths(jax.random.fold_in(arg_keys[10], 71), 0)
    dest = draw_dest(jax.random.fold_in(arg_keys[10], 71), 0)
    return dict(x_slots=x_slots, gain=gain, adapter=adapter, readout=readout, drift=drift, ref_gap=ref_gap, rewards=rewards, groups=groups, lengths=lengths, dest=dest)


kl_coef = 0.1
norm_eps = 1e-06
upper_log = math.log(1.2)
lower_log = math.log(0.8)

def advantages(rewards, groups):
    same_group = (groups[..., :, None] == groups[..., None, :]).astype(rewards.dtype)
    members = lax.optimization_barrier(jnp.sum(same_group, -1))
    group_mean = lax.optimization_barrier(jnp.sum(same_group * rewards[..., None, :], -1)) / members
    spread = lax.optimization_barrier(jnp.sum(same_group * (rewards[..., None, :] - group_mean[..., :, None]) ** 2, -1)) / members
    return (rewards - group_mean) / jnp.sqrt(jnp.maximum(spread, 0.25))

def latent_grad(latent, readout_rows, drift_rows, gap_rows, adv_rows, weight):
    readout_f = readout_rows.astype(jnp.float32)
    shift_value = lax.optimization_barrier(jnp.sum(latent * readout_f, -1))
    logratio = drift_rows + shift_value
    ratio_value = jnp.exp(logratio)
    upper = jnp.asarray(upper_log, drift_rows.dtype)
    lower = jnp.asarray(lower_log, drift_rows.dtype)
    keep_mask = jnp.where(adv_rows >= 0, drift_rows <= upper, drift_rows >= lower).astype(drift_rows.dtype)
    dshift = weight * (-adv_rows * ratio_value * keep_mask + kl_coef * (1.0 - jnp.exp(gap_rows - logratio)))
    return (dshift[:, None] * readout_f).astype(jnp.bfloat16)

def reference(x_slots, gain, adapter, readout, drift, ref_gap, rewards, groups, lengths, dest):
    advantage = advantages(rewards, groups)
    roll_index = (jnp.arange(SLOTS) // LMAX).astype(jnp.int32)
    slot_position = (jnp.arange(SLOTS) % LMAX).astype(jnp.int32)
    gain_f = gain.astype(jnp.float32)

    def column(running_total, column_items):
        x_col, read_col, drift_col, gap_col, adv_col, len_col, dest_col = column_items
        rank_ids = jnp.arange(N_DP).astype(jnp.int32)
        rank_tokens = lax.optimization_barrier(jnp.sum(jnp.where(dest_col[None, :] == rank_ids[:, None], len_col[None, :], 0), 1))
        slot_len = len_col[roll_index]
        live_slot = slot_position < slot_len
        slot_tokens = rank_tokens[dest_col[roll_index]].astype(jnp.float32)
        weight = jnp.where(live_slot, 1.0 / slot_tokens, jnp.zeros((), jnp.float32))
        adv_slot = adv_col[roll_index]
        x_float = x_col.astype(jnp.float32)
        normed = x_float * lax.rsqrt(lax.optimization_barrier(jnp.mean(x_float * x_float, -1, keepdims=True)) + norm_eps)
        zb = (normed * gain_f).astype(jnp.bfloat16)
        latent = jnp.dot(zb, adapter, preferred_element_type=jnp.float32)
        dlatent = latent_grad(latent, read_col, drift_col, gap_col, adv_slot, weight)
        term = lax.dot_general(zb, dlatent, (((0,), (0,)), ((), ())), preferred_element_type=jnp.float32)
        return (running_total + term, None)
    grad_adapter, unused = lax.scan(column, jnp.zeros((D, R), jnp.float32), (x_slots, readout, drift, ref_gap, advantage, lengths, dest))
    grad_gain = lax.optimization_barrier(jnp.sum(adapter.astype(jnp.float32) * grad_adapter, 1)) / gain_f
    return (grad_adapter, grad_gain)
```

```python
import math

import jax
import jax.numpy as jnp
from jax import lax
from jax.experimental import pallas as pl
from jax.experimental.pallas import tpu as pltpu
from jax.sharding import PartitionSpec as P

WIDTH = 4608
RANK = 256
SLOTS = 3072
LMAX = 64
ROLLS = 48
NP = 16
NZ = 12
NX = 4
FEAT = WIDTH // NP
BLOCK = WIDTH // (NZ * NX)
PER = FEAT // BLOCK
CHUNK = 256
NCH = SLOTS // CHUNK
TILES = 12
kl_coef = 0.1
norm_eps = 1e-06
upper_log = math.log(1.2)
lower_log = math.log(0.8)
F32 = jnp.float32
BF16 = jnp.bfloat16
MESH = pl.DeviceIdType.MESH


def rcopy(src, dst, ssem, rsem, dev):
    return pltpu.make_async_remote_copy(
        src_ref=src, dst_ref=dst, send_sem=ssem, recv_sem=rsem, device_id=dev, device_id_type=MESH
    )


def loop(n, f, start=0):
    def step(i, carry):
        f(i)
        return carry

    lax.fori_loop(start, n, step, jnp.int32(0))


def eye(n, dtype=F32):
    r = lax.broadcasted_iota(jnp.int32, (n, n), 0)
    c = lax.broadcasted_iota(jnp.int32, (n, n), 1)
    return (r == c).astype(F32).astype(dtype)


def contract_last(a, b):
    return lax.dot_general(a, b, (((1,), (1,)), ((), ())), preferred_element_type=F32)


def kernel(
    x_h, gain_h, ad_h, ro_h, drift_h, gap_h, rew_h, grp_h, len_h, dst_h,
    grad_o, ggain_o,
    xv, rv, adv, gainv, driftv, gapv, rewv, grpv, lenv, dstv,
    xT, rT, zT, dT, W, gfull,
    ssp, ssr, rsv, qp, qr, wv,
    AZ, AX, CXs, CX, Sf, CZs, CZ, CD, CF,
    lsem, xsem,
    sAZ, rAZ, sAD, rAD, sAX, rAX,
    sS, rS, sR, rR, sQ, rQ, sW, rW,
    sCX, rCX, sCZ, rCZ, sCD, rCD, sCF, rCF,
):
    p = lax.axis_index("dp")
    c = lax.axis_index("fsdp")
    z = c // NX
    x = c % NX
    kp = jnp.minimum(p, NCH - 1)

    def zdev(z2):
        return (p, z2 * NX + x)

    def xdev(x2):
        return (p, z * NX + x2)

    def ddev(p2):
        return (p2, c)

    def act(x2):
        return lax.rem(x2 + p, 4) != 3

    active = act(x)
    holder = p <= TILES
    owner = p < NCH

    small = [
        (ad_h, adv), (gain_h, gainv), (drift_h, driftv), (gap_h, gapv), (rew_h, rewv),
        (grp_h, grpv), (len_h, lenv), (dst_h, dstv), (ro_h.at[0], rv),
    ]
    loads = [pltpu.make_async_copy(s, d, lsem.at[i]) for i, (s, d) in enumerate(small)]
    XS = SLOTS // 4
    xloads = [
        pltpu.make_async_copy(x_h.at[0, pl.ds(i * XS, XS)], xv.at[pl.ds(i * XS, XS)], xsem.at[i])
        for i in range(4)
    ]
    for d in loads[:2]:
        d.start()
    for d in xloads:
        d.start()
    for d in loads[2:]:
        d.start()

    barrier = pltpu.get_barrier_semaphore()

    def greet(dev):
        pl.semaphore_signal(barrier, inc=1, device_id=dev, device_id_type=MESH)

    loop(NZ, lambda d: greet(zdev(lax.rem(z + d, NZ))), 1)
    loop(NX, lambda d: greet(xdev(lax.rem(x + d, NX))), 1)
    loop(NP, lambda d: greet(ddev(lax.rem(p + d, NP))), 1)
    for d in loads[:2]:
        d.wait()

    for k in range(TILES):
        @pl.when(p == k)
        def _(k=k):
            AZ[z] = adv[16 * (k // 2):16 * (k // 2) + 16, 128 * (k % 2):128 * (k % 2) + 128]

    @pl.when(p == TILES)
    def _():
        row = jnp.concatenate([gainv[...].astype(F32), jnp.ones((1, 128 - BLOCK), F32)], axis=1)
        AZ[z] = jnp.broadcast_to(row, (16, 128)).astype(BF16)

    pl.semaphore_wait(barrier, NZ + NX + NP - 3)

    def az(d):
        return rcopy(AZ.at[z], AZ.at[z], sAZ.at[d], rAZ.at[z], zdev(lax.rem(z + d, NZ)))

    @pl.when(holder)
    def _():
        loop(NZ, lambda d: az(d).start(), 1)

    ident = eye(FEAT, BF16)
    for q in range(4):
        xloads[q].wait()

        def tchunk(i):
            xt = contract_last(ident, xv[pl.ds(pl.multiple_of(i * CHUNK, CHUNK), CHUNK), :])
            xT[i] = xt
            ssp[i] = jnp.sum(xt * xt, axis=0, keepdims=True)

        loop((q + 1) * NCH // 4, tchunk, q * NCH // 4)

    def scatter(part, slots, ss, rs):
        def one(k):
            @pl.when(k != p)
            def _():
                rcopy(part.at[k], slots.at[p], ss.at[k], rs.at[p], ddev(k)).start()
        return one

    loop(NCH, scatter(ssp, ssr, sS, rS))

    def ad_of(zz):
        p2 = (NX * zz + x) // PER
        return p2, rcopy(AZ.at[zz], AX.at[x, p], sAD.at[zz], rAD.at[p], ddev(p2))

    def az_in(zz):
        return rcopy(AZ.at[zz], AZ.at[zz], sAZ.at[0], rAZ.at[zz], zdev(lax.rem(z + 1, NZ)))

    @pl.when(holder)
    def _():
        def step(i):
            zz = lax.rem(z + i, NZ)

            @pl.when(i > 0)
            def _():
                az_in(zz).wait_recv()

            p2, d = ad_of(zz)

            @pl.when(p2 != p)
            def _():
                d.start()

            @pl.when(p2 == p)
            def _():
                AX[x, p] = AZ[zz]

        loop(NZ, step)

    for d in loads[2:]:
        d.wait()
    ident_r = eye(RANK, BF16)

    def rchunk(i):
        rT[i] = contract_last(
            ident_r, rv[pl.ds(pl.multiple_of(i * CHUNK, CHUNK), CHUNK), :]
        ).astype(BF16)

    loop(NCH, rchunk)

    def gathered(part, slots, rs):
        def one(d):
            p2 = lax.rem(p + d, NP)
            rcopy(slots.at[p2], slots.at[p2], rs.at[p2], rs.at[p2], ddev(p2)).wait_recv()

        loop(NP, one, 1)
        slots[p] = part[kp]
        total = slots[0]
        for i in range(1, NP):
            total = total + slots[i]
        return total

    def spread_all(buf, ss, rs):
        def one(d):
            rcopy(buf.at[p], buf.at[p], ss.at[d], rs.at[p], ddev(lax.rem(p + d, NP))).start()
        loop(NP, one, 1)

    def spread_wait(buf, rs):
        def one(k):
            @pl.when(k != p)
            def _():
                rcopy(buf.at[k], buf.at[k], rs.at[k], rs.at[k], ddev(lax.rem(p + 1, NP))).wait_recv()
        loop(NCH, one)

    @pl.when(owner)
    def _():
        total = gathered(ssp, ssr, rS)
        rsv[p] = lax.rsqrt(total * (1.0 / WIDTH) + norm_eps)
        spread_all(rsv, sR, rR)

    def ax(d):
        return rcopy(AX.at[x], AX.at[x], sAX.at[d], rAX.at[x], xdev(lax.rem(x + d, NX)))

    @pl.when(active)
    def _():
        def one(k):
            @pl.when(k != p)
            def _():
                rcopy(AX.at[x, k], AX.at[x, k], rAD.at[k], rAD.at[k], ddev(lax.rem(p + 1, NP))).wait_recv()
        loop(TILES + 1, one)
        loop(NX, lambda d: ax(d).start(), 1)

    e48 = eye(ROLLS)

    def col(row):
        return jnp.sum(e48 * row, axis=1, keepdims=True)

    rew = rewv[...]
    grp = grpv[...].astype(F32)
    dst = dstv[...].astype(F32)
    ln = lenv[...].astype(F32)
    rew_c, len_c = col(rew), col(ln)
    same = (col(grp) == grp).astype(F32)
    members = jnp.sum(same, axis=0, keepdims=True)
    mean = jnp.sum(same * rew_c, axis=0, keepdims=True) / members
    var = jnp.sum(same * (rew_c - mean) ** 2, axis=0, keepdims=True) / members
    advantage = (rew - mean) / jnp.sqrt(jnp.maximum(var, 0.25))
    tokens = jnp.sum((col(dst) == dst).astype(F32) * len_c, axis=0, keepdims=True)
    inv = 1.0 / tokens
    slot = lax.broadcasted_iota(jnp.int32, (ROLLS, CHUNK), 1)
    roll = lax.broadcasted_iota(jnp.int32, (ROLLS, CHUNK), 0)
    pick = (roll == slot // LMAX + kp * (CHUNK // LMAX)).astype(F32)

    def expand(column):
        return jnp.sum(pick * column, axis=0, keepdims=True)

    adv_s = expand(col(advantage))
    inv_s = expand(col(inv))
    len_s = expand(len_c)
    place = lax.rem(lax.broadcasted_iota(jnp.int32, (1, CHUNK), 1), LMAX).astype(F32)
    live = place < len_s

    spread_wait(rsv, rR)

    def nchunk(i):
        xT[i] = xT[i] * rsv[i]

    loop(NCH, nchunk)

    for x2 in range(NX):
        @pl.when((x2 != x) & act(x2))
        def _(x2=x2):
            rcopy(AX.at[x2], AX.at[x2], rAX.at[x2], rAX.at[x2], xdev(lax.rem(x + 1, NX))).wait_recv()

    e96 = eye(BLOCK)
    for j in range(PER):
        xs = lax.rem(j + 3 * p, 4)
        for k in range(TILES):
            r0 = BLOCK * j + 16 * (k // 2)
            W[r0:r0 + 16, 128 * (k % 2):128 * (k % 2) + 128] = AX[xs, k]
        grow = AX[xs, TILES].astype(F32)[0:1, 0:BLOCK]
        gfull[BLOCK * j:BLOCK * j + BLOCK, :] = jnp.broadcast_to(
            jnp.sum(e96 * grow, axis=1, keepdims=True), (BLOCK, CHUNK)
        )

    send_q = scatter(qp, qr, sQ, rQ)

    def qchunk(i):
        h = jnp.dot(W[...], rT[i], preferred_element_type=F32)
        zb = (xT[i] * gfull[...]).astype(BF16)
        zT[i] = zb
        qp[i] = jnp.sum(zb.astype(F32) * h, axis=0, keepdims=True)
        send_q(i)

    loop(NCH, qchunk)

    @pl.when(owner)
    def _():
        shift = gathered(qp, qr, rQ)
        drift = driftv[:, pl.ds(pl.multiple_of(kp * CHUNK, CHUNK), CHUNK)]
        gap = gapv[:, pl.ds(pl.multiple_of(kp * CHUNK, CHUNK), CHUNK)]
        logratio = drift + shift
        ratio = jnp.exp(logratio)
        keep = jnp.where(
            adv_s >= 0,
            (drift <= jnp.float32(upper_log)).astype(F32),
            (drift >= jnp.float32(lower_log)).astype(F32),
        )
        dshift = inv_s * (-adv_s * ratio * keep + kl_coef * (1.0 - jnp.exp(gap - logratio)))
        wv[p] = jnp.where(live, dshift, 0.0)
        spread_all(wv, sW, rW)

    spread_wait(wv, rW)

    def dchunk(i):
        dT[i] = (rT[i].astype(F32) * wv[i]).astype(BF16)

    loop(NCH, dchunk)
    g = contract_last(zT[0], dT[0])
    for i in range(1, NCH):
        g = g + contract_last(zT[i], dT[i])
    for j in range(PER):
        for k in range(TILES):
            r0 = BLOCK * j + 16 * (k // 2)
            CXs[j, k] = g[r0:r0 + 16, 128 * (k % 2):128 * (k % 2) + 128].astype(BF16)

    def cx(j):
        xs = lax.rem(j + 3 * p, 4)
        return xs, rcopy(CXs.at[j], CX.at[x], sCX.at[j], rCX.at[x], xdev(xs))

    for j in range(PER):
        xs, d = cx(j)

        @pl.when(xs != x)
        def _(d=d):
            d.start()

        @pl.when(xs == x)
        def _(j=j):
            CX[x] = CXs[j]

    def cz(d):
        z2 = lax.rem(z + d, NZ)
        return rcopy(CZs.at[z2], CZ.at[z], sCZ.at[d], rCZ.at[z], zdev(z2))

    def cd(d):
        return rcopy(CD.at[p], CD.at[p], sCD.at[d], rCD.at[p], ddev(lax.rem(p + d, NP)))

    @pl.when(active)
    def _():
        def cx_in(d):
            x2 = lax.rem(x + d, NX)
            rcopy(CX.at[x2], CX.at[x2], rCX.at[x2], rCX.at[x2], xdev(x2)).wait_recv()

        loop(NX, cx_in, 1)
        total = CX[0].astype(F32)
        for i in range(1, NX):
            total = total + CX[i].astype(F32)
        Sf[...] = total
        CZs[...] = total.astype(BF16)
        loop(NZ, lambda d: cz(d).start(), 1)
        CZ[z] = jnp.zeros((16, 128), BF16)

        def cz_in(d):
            z2 = lax.rem(z + d, NZ)
            rcopy(CZ.at[z2], CZ.at[z2], rCZ.at[z2], rCZ.at[z2], zdev(z2)).wait_recv()

        loop(NZ, cz_in, 1)
        tile = Sf[z]
        for i in range(NZ):
            tile = tile + CZ[i].astype(F32)
        CD[p] = tile.astype(BF16)
        loop(NP, lambda d: cd(d).start(), 1)

    def cf(zz):
        p2 = (NX * zz + x) // PER
        return p2, rcopy(CD.at[p2], CF.at[z], sCF.at[zz], rCF.at[z], zdev(zz))

    def cfstep(zz):
        p2, d = cf(zz)

        @pl.when(p2 != p)
        def _():
            rcopy(CD.at[p2], CD.at[p2], rCD.at[p2], rCD.at[p2], ddev(lax.rem(p + 1, NP))).wait_recv()

        @pl.when(zz != z)
        def _():
            d.start()

        @pl.when(zz == z)
        def _():
            CF[z] = CD[p2]

    loop(NZ, cfstep)

    def cf_in(d):
        z2 = lax.rem(z + d, NZ)
        rcopy(CF.at[z2], CF.at[z2], rCF.at[z2], rCF.at[z2], zdev(z2)).wait_recv()

    loop(NZ, cf_in, 1)
    for k in range(TILES):
        r0, c0 = 16 * (k // 2), 128 * (k % 2)
        grad_o[r0:r0 + 16, c0:c0 + 128] = CF[k].astype(F32)
    gsum = jnp.sum(grad_o[...] * adv[...].astype(F32), axis=1, keepdims=True)
    ggain_o[...] = jnp.sum(e96 * gsum, axis=0, keepdims=True) / gainv[...].astype(F32)

    @pl.when(holder)
    def _():
        loop(NZ, lambda d: az(d).wait_send(), 1)

        def one(zz):
            p2, d = ad_of(zz)

            @pl.when(p2 != p)
            def _():
                d.wait_send()

        loop(NZ, one)

    @pl.when(active)
    def _():
        loop(NX, lambda d: ax(d).wait_send(), 1)
        loop(NZ, lambda d: cz(d).wait_send(), 1)
        loop(NP, lambda d: cd(d).wait_send(), 1)

    def scattered(part, slots, ss, rs):
        def one(k):
            @pl.when(k != p)
            def _():
                rcopy(part.at[k], slots.at[p], ss.at[k], rs.at[p], ddev(k)).wait_send()
        return one

    loop(NCH, scattered(ssp, ssr, sS, rS))
    loop(NCH, scattered(qp, qr, sQ, rQ))

    @pl.when(owner)
    def _():
        def one(d):
            p2 = lax.rem(p + d, NP)
            rcopy(rsv.at[p], rsv.at[p], sR.at[d], rR.at[p], ddev(p2)).wait_send()
            rcopy(wv.at[p], wv.at[p], sW.at[d], rW.at[p], ddev(p2)).wait_send()
        loop(NP, one, 1)

    for j in range(PER):
        xs, d = cx(j)

        @pl.when(xs != x)
        def _(d=d):
            d.wait_send()

    def cfout(d):
        cf(lax.rem(z + d, NZ))[1].wait_send()

    loop(NZ, cfout, 1)


def per_device(x_slots, gain, adapter, readout, drift, ref_gap, rewards, groups, lengths, dest):
    V = pltpu.VMEM
    D = pltpu.SemaphoreType.DMA
    any_spec = pl.BlockSpec(memory_space=pl.ANY)
    vmem_spec = pl.BlockSpec(memory_space=pltpu.VMEM)
    grad, ggain = pl.pallas_call(
        kernel,
        out_shape=(
            jax.ShapeDtypeStruct((BLOCK, RANK), F32),
            jax.ShapeDtypeStruct((1, BLOCK), F32),
        ),
        in_specs=[any_spec] * 10,
        out_specs=(vmem_spec, vmem_spec),
        scratch_shapes=[
            V((SLOTS, FEAT), BF16), V((SLOTS, RANK), BF16), V((BLOCK, RANK), BF16), V((1, BLOCK), BF16),
            V((1, SLOTS), F32), V((1, SLOTS), F32), V((1, ROLLS), F32),
            V((1, ROLLS), jnp.int32), V((1, ROLLS), jnp.int32), V((1, ROLLS), jnp.int32),
            V((NCH, FEAT, CHUNK), F32), V((NCH, RANK, CHUNK), BF16), V((NCH, FEAT, CHUNK), BF16),
            V((NCH, RANK, CHUNK), BF16), V((FEAT, RANK), BF16), V((FEAT, CHUNK), F32),
            V((NCH, 1, CHUNK), F32), V((NP, 1, CHUNK), F32), V((NCH, 1, CHUNK), F32),
            V((NCH, 1, CHUNK), F32), V((NP, 1, CHUNK), F32), V((NCH, 1, CHUNK), F32),
            V((NZ, 16, 128), BF16), V((NX, TILES + 1, 16, 128), BF16),
            V((PER, TILES, 16, 128), BF16), V((NX, TILES, 16, 128), BF16),
            V((TILES, 16, 128), F32), V((TILES, 16, 128), BF16), V((NZ, 16, 128), BF16),
            V((NP, 16, 128), BF16), V((NZ, 16, 128), BF16),
            D((9,)), D((4,)),
            D((NZ,)), D((NZ,)), D((NZ,)), D((NP,)), D((NX,)), D((NX,)),
            D((NP,)), D((NP,)), D((NP,)), D((NP,)), D((NP,)), D((NP,)), D((NP,)), D((NP,)),
            D((NX,)), D((NX,)), D((NZ,)), D((NZ,)), D((NP,)), D((NP,)), D((NZ,)), D((NZ,)),
        ],
        compiler_params=pltpu.CompilerParams(
            collective_id=0, has_side_effects=True, vmem_limit_bytes=48 * 1024 * 1024
        ),
    )(
        x_slots, gain.reshape(1, BLOCK), adapter, readout, drift, ref_gap, rewards, groups, lengths,
        dest,
    )
    return grad, ggain.reshape(BLOCK)


def solution(mesh):
    in_specs = (
        P("fsdp", None, "dp"),
        P("fsdp"),
        P("fsdp", None),
        P("fsdp", None, None),
        P("fsdp", None),
        P("fsdp", None),
        P("fsdp", None),
        P("fsdp", None),
        P("fsdp", None),
        P("fsdp", None),
    )
    out_specs = (P("fsdp", None), P("fsdp"))
    return jax.shard_map(
        per_device, mesh=mesh, in_specs=in_specs, out_specs=out_specs, check_vma=False
    )
```

```python
import math

import jax
import jax.numpy as jnp
from jax import lax
from jax.experimental import pallas as pl
from jax.experimental.pallas import tpu as pltpu
from jax.sharding import PartitionSpec as P

WIDTH = 4608
RANK = 256
SLOTS = 3072
LMAX = 64
ROLLS = 48
NP = 16
NZ = 12
NX = 4
FEAT = WIDTH // NP
BLOCK = WIDTH // (NZ * NX)
PER = FEAT // BLOCK
CHUNK = 256
NCH = SLOTS // CHUNK
TILES = 12
HALF = NCH // 2
GROUP = 4
FAR_Z = (6, 5, 7, 4, 8, 3, 9, 2, 10, 1, 11)
FAR_Y = (4, 3, 5, 2, 6, 1, 7)
FAR_P = (8, 7, 9, 6, 10, 5, 11, 4, 12, 3, 13, 2, 14, 1, 15)
kl_coef = 0.1
norm_eps = 1e-06
upper_log = math.log(1.2)
lower_log = math.log(0.8)
F32 = jnp.float32
BF16 = jnp.bfloat16
MESH = pl.DeviceIdType.MESH


def rcopy(src, dst, ssem, rsem, dev):
    return pltpu.make_async_remote_copy(
        src_ref=src, dst_ref=dst, send_sem=ssem, recv_sem=rsem, device_id=dev, device_id_type=MESH
    )


def loop(n, f, start=0):
    def step(i, carry):
        f(i)
        return carry

    lax.fori_loop(start, n, step, jnp.int32(0))


def eye(n, dtype=F32):
    r = lax.broadcasted_iota(jnp.int32, (n, n), 0)
    c = lax.broadcasted_iota(jnp.int32, (n, n), 1)
    return (r == c).astype(F32).astype(dtype)


def contract_last(a, b):
    return lax.dot_general(a, b, (((1,), (1,)), ((), ())), preferred_element_type=F32)


def kernel(
    x_h, gain_h, ad_h, ro_h, drift_h, gap_h, rew_h, grp_h, len_h, dst_h,
    grad_o, ggain_o,
    xv, rv, adv, gainv, driftv, gapv, rewv, grpv, lenv, dstv,
    rT, zT, dT, W, gfull,
    ssp, ssr, ssy, rsv, qp, qr, qy, wv, adv_s, inv_s, len_s,
    AZ, AX, CXs, CX, CZs, CM, CD,
    lsem, xsem,
    sAZ, rAZ, sAD, rAD, sAX, rAX,
    sS, rS, sQ, rQ,
    sCX, rCX, sCM, rCM, sCD, rCD,
):
    p = lax.axis_index("dp")
    c = lax.axis_index("fsdp")
    z = c // NX
    x = c % NX
    y = p // 2
    core = p % 2
    mine = core * HALF
    theirs = (1 - core) * HALF

    def zdev(z2):
        return (p, z2 * NX + x)

    def xdev(x2):
        return (p, z * NX + x2)

    def ddev(p2):
        return (p2, c)

    def act(x2):
        return lax.rem(x2 + p, 4) != 3

    sibling = (p + 1 - 2 * core, c)
    active = act(x)
    holder = p <= TILES
    owner = p < TILES

    small = [
        (ad_h, adv), (gain_h, gainv), (ro_h.at[0], rv), (drift_h, driftv), (gap_h, gapv), (rew_h, rewv),
        (grp_h, grpv), (len_h, lenv), (dst_h, dstv),
    ]
    loads = [pltpu.make_async_copy(s, d, lsem.at[i]) for i, (s, d) in enumerate(small)]
    xload = pltpu.make_async_copy(x_h, xv, xsem.at[0])
    loads[0].start()
    loads[1].start()
    xload.start()
    for d in loads[2:]:
        d.start()

    barrier = pltpu.get_barrier_semaphore()

    def greet(dev):
        pl.semaphore_signal(barrier, inc=1, device_id=dev, device_id_type=MESH)

    for d in FAR_Z:
        greet(zdev(lax.rem(z + d, NZ)))
    for d in FAR_Y:
        for k in range(2):
            greet(ddev(lax.rem(y + d, 8) * 2 + k))
    for d in (2, 1, 3):
        greet(xdev(lax.rem(x + d, NX)))
    greet(sibling)
    loads[0].wait()
    loads[1].wait()

    for k in range(TILES):
        @pl.when(p == k)
        def _(k=k):
            AZ[z] = adv[16 * (k // 2):16 * (k // 2) + 16, 128 * (k % 2):128 * (k % 2) + 128]

    @pl.when(p == TILES)
    def _():
        row = jnp.concatenate([gainv[...].astype(F32), jnp.ones((1, 128 - BLOCK), F32)], axis=1)
        AZ[z] = jnp.broadcast_to(row, (16, 128)).astype(BF16)

    xload.wait()
    for i in range(NCH):
        xt = xv[:, i * CHUNK:(i + 1) * CHUNK].astype(F32)
        ssp[i] = jnp.sum(xt * xt, axis=0, keepdims=True)

    pl.semaphore_wait(barrier, NZ + NX + NP - 3)

    def az(d):
        return rcopy(AZ.at[z], AZ.at[z], sAZ.at[d], rAZ.at[z], zdev(lax.rem(z + d, NZ)))

    @pl.when(holder)
    def _():
        for d in FAR_Z:
            az(d).start()

    def pair(src, dst, ss, rs, i):
        return rcopy(src, dst, ss.at[i], rs.at[i], sibling)

    def pair_half(part, got, ss, rs):
        return pair(part.at[pl.ds(theirs, HALF)], got, ss, rs, 8)

    def y_send(ys, ss, rs, d):
        return rcopy(ys.at[y], ys.at[y], ss.at[d], rs.at[y], ddev(lax.rem(y + d, 8) * 2 + core))

    def y_start(part, got, ys, ss, rs):
        pair_half(part, got, ss, rs).wait_recv()
        ys[y] = part[pl.ds(mine, HALF)] + got[...]
        for d in FAR_Y:
            y_send(ys, ss, rs, d).start()

    def y_sum(ys, ss, rs):
        for d in range(1, 8):
            y2 = lax.rem(y + d, 8)
            rcopy(ys.at[y2], ys.at[y2], ss.at[d], rs.at[y2], sibling).wait_recv()
        total = ys[0]
        for i in range(1, 8):
            total = total + ys[i]
        return total

    def pair_back(out, ss, rs):
        part = out.at[pl.ds(mine, HALF)]
        return pair(part, part, ss, rs, 9)

    def pair_back_in(out, ss, rs):
        part = out.at[pl.ds(theirs, HALF)]
        return pair(part, part, ss, rs, 9)

    pair_half(ssp, ssr, sS, rS).start()

    for d in loads[2:]:
        d.wait()
    ident = eye(RANK, BF16)
    for i in range(NCH):
        rT[i] = contract_last(ident, rv[i * CHUNK:(i + 1) * CHUNK, :]).astype(BF16)

    y_start(ssp, ssr, ssy, sS, rS)

    e48 = eye(ROLLS)

    def col(row):
        return jnp.sum(e48 * row, axis=1, keepdims=True)

    rew = rewv[...]
    grp = grpv[...].astype(F32)
    dst = dstv[...].astype(F32)
    ln = lenv[...].astype(F32)
    rew_c, len_c = col(rew), col(ln)
    same = (col(grp) == grp).astype(F32)
    members = jnp.sum(same, axis=0, keepdims=True)
    mean = jnp.sum(same * rew_c, axis=0, keepdims=True) / members
    var = jnp.sum(same * (rew_c - mean) ** 2, axis=0, keepdims=True) / members
    advantage = (rew - mean) / jnp.sqrt(jnp.maximum(var, 0.25))
    tokens = jnp.sum((col(dst) == dst).astype(F32) * len_c, axis=0, keepdims=True)
    adv_c, inv_c = col(advantage), col(1.0 / tokens)
    slot = lax.broadcasted_iota(jnp.int32, (ROLLS, CHUNK), 1)
    roll = lax.broadcasted_iota(jnp.int32, (ROLLS, CHUNK), 0)
    for i in range(HALF):
        pick = (roll == slot // LMAX + (mine + i) * (CHUNK // LMAX)).astype(F32)
        adv_s[i] = jnp.sum(pick * adv_c, axis=0, keepdims=True)
        inv_s[i] = jnp.sum(pick * inv_c, axis=0, keepdims=True)
        len_s[i] = jnp.sum(pick * len_c, axis=0, keepdims=True)

    def ad_of(zz):
        p2 = (NX * zz + x) // PER
        return p2, rcopy(AZ.at[zz], AX.at[x, p], sAD.at[zz], rAD.at[p], ddev(p2))

    @pl.when(holder)
    def _():
        for i in (0,) + FAR_Z[::-1]:
            zz = lax.rem(z + i, NZ)
            if i > 0:
                rcopy(AZ.at[zz], AZ.at[zz], sAZ.at[0], rAZ.at[zz], sibling).wait_recv()
            p2, d = ad_of(zz)

            @pl.when(p2 != p)
            def _(d=d):
                d.start()

            @pl.when(p2 == p)
            def _(zz=zz):
                AX[x, p] = AZ[zz]

    total = y_sum(ssy, sS, rS)
    rsv[pl.ds(mine, HALF)] = lax.rsqrt(total * (1.0 / WIDTH) + norm_eps)
    pair_back(rsv, sS, rS).start()

    def ax(k, d):
        return rcopy(AX.at[x, k], AX.at[x, k], sAX.at[d], rAX.at[x], xdev(lax.rem(x + d, NX)))

    @pl.when(active)
    def _():
        def one(i):
            m = i // 2
            dy = jnp.where(lax.rem(m, 2) == 1, (m + 1) // 2, 8 - m // 2)
            k = lax.rem(y + dy, 8) * 2 + lax.rem(i, 2)

            @pl.when(k <= TILES)
            def _():
                @pl.when(k != p)
                def _():
                    rcopy(AX.at[x, k], AX.at[x, k], rAD.at[k], rAD.at[k], sibling).wait_recv()
                for d in (2, 1, 3):
                    ax(k, d).start()
        loop(NP, one)

    pair_back_in(rsv, sS, rS).wait_recv()
    for x2 in range(NX):
        @pl.when((x2 != x) & act(x2))
        def _(x2=x2):
            rcopy(AX.at[x2], AX.at[x2], rAX.at[x2], rAX.at[x2], sibling).wait_recv()

    e96 = eye(BLOCK)
    for j in range(PER):
        xs = lax.rem(j + 3 * p, 4)
        for k in range(TILES):
            r0 = BLOCK * j + 16 * (k // 2)
            W[r0:r0 + 16, 128 * (k % 2):128 * (k % 2) + 128] = AX[xs, k]
        grow = AX[xs, TILES].astype(F32)[0:1, 0:BLOCK]
        gfull[BLOCK * j:BLOCK * j + BLOCK, :] = jnp.broadcast_to(
            jnp.sum(e96 * grow, axis=1, keepdims=True), (BLOCK, CHUNK)
        )

    def qchunk(i):
        at = pl.multiple_of(i * CHUNK, CHUNK)
        h = contract_last(W[...], rv[pl.ds(at, CHUNK), :])
        zb = (xv[:, pl.ds(at, CHUNK)].astype(F32) * rsv[i] * gfull[...]).astype(BF16)
        zT[i] = zb
        qp[i] = jnp.sum(zb.astype(F32) * h, axis=0, keepdims=True)

    for i in range(HALF):
        qchunk(theirs + i)
    pair_half(qp, qr, sQ, rQ).start()
    for i in range(HALF):
        qchunk(mine + i)
    y_start(qp, qr, qy, sQ, rQ)
    shift = y_sum(qy, sQ, rQ)
    drift = driftv[pl.ds(mine, HALF)]
    gap = gapv[pl.ds(mine, HALF)]
    adv_rows = adv_s[...]
    logratio = drift + shift
    ratio = jnp.exp(logratio)
    keep = jnp.where(
        adv_rows >= 0,
        (drift <= jnp.float32(upper_log)).astype(F32),
        (drift >= jnp.float32(lower_log)).astype(F32),
    )
    dshift = inv_s[...] * (-adv_rows * ratio * keep + kl_coef * (1.0 - jnp.exp(gap - logratio)))
    place = lax.rem(lax.broadcasted_iota(jnp.int32, (HALF, 1, CHUNK), 2), LMAX).astype(F32)
    wv[pl.ds(mine, HALF)] = jnp.where(place < len_s[...], dshift, 0.0)
    pair_back(wv, sQ, rQ).start()
    for i in range(HALF):
        dT[mine + i] = (rT[mine + i].astype(F32) * wv[mine + i]).astype(BF16)
    pair_back_in(wv, sQ, rQ).wait_recv()
    for i in range(HALF):
        dT[theirs + i] = (rT[theirs + i].astype(F32) * wv[theirs + i]).astype(BF16)

    g = contract_last(zT[0], dT[0])
    for i in range(1, NCH):
        g = g + contract_last(zT[i], dT[i])
    for j in range(PER):
        for k in range(TILES):
            r0 = BLOCK * j + 16 * (k // 2)
            CXs[j, k] = g[r0:r0 + 16, 128 * (k % 2):128 * (k % 2) + 128].astype(BF16)

    def cx(j, s):
        xs = lax.rem(j + 3 * p, 4)
        part = pl.ds(GROUP * s, GROUP)
        return xs, rcopy(CXs.at[j, part], CX.at[x, part], sCX.at[j, s], rCX.at[x, s], xdev(xs))

    for s in range(TILES // GROUP):
        for j in range(PER):
            xs, d = cx(j, s)

            @pl.when(xs != x)
            def _(d=d):
                d.start()

    for j in range(PER):
        @pl.when(lax.rem(j + 3 * p, 4) == x)
        def _(j=j):
            CX[x] = CXs[j]

    block = PER * p + jnp.minimum(lax.rem(x + p, 4), PER - 1)
    at_home = block // NX == z

    def cm(k):
        return rcopy(CZs.at[k], CM.at[z], sCM.at[k], rCM.at[z], (k, block))

    @pl.when(active)
    def _():
        for s in range(TILES // GROUP):
            part = pl.ds(GROUP * s, GROUP)
            for d in (1, 3, 2):
                x2 = lax.rem(x + d, NX)
                rcopy(CX.at[x2, part], CX.at[x2, part], rCX.at[x2, s], rCX.at[x2, s], sibling).wait_recv()
            total = CX[0, part].astype(F32)
            for i in range(1, NX):
                total = total + CX[i, part].astype(F32)
            CZs[part] = total.astype(BF16)
            for k in range(GROUP * s, GROUP * s + GROUP):
                @pl.when(jnp.logical_not(at_home & (p == k)))
                def _(k=k):
                    cm(k).start()

                @pl.when(at_home & (p == k))
                def _(k=k):
                    CM[z] = CZs[k]

    feeder = c // PER

    def cd(d):
        return rcopy(CD.at[p], CD.at[p], sCD.at[d], rCD.at[p], ddev(lax.rem(p + d, NP)))

    @pl.when(owner)
    def _():
        for d in (0,) + FAR_Z[::-1]:
            zz = lax.rem(z + d, NZ)

            def arrive(zz=zz):
                rcopy(CM.at[zz], CM.at[zz], rCM.at[zz], rCM.at[zz], sibling).wait_recv()

            if d == 0:
                pl.when(feeder != p)(arrive)
            else:
                arrive()
        tile = CM[0].astype(F32)
        for i in range(1, NZ):
            tile = tile + CM[i].astype(F32)
        CD[p] = tile.astype(BF16)
        for d in FAR_P:
            cd(d).start()

    for k in range(TILES):
        @pl.when(p != k)
        def _(k=k):
            rcopy(CD.at[k], CD.at[k], rCD.at[k], rCD.at[k], sibling).wait_recv()
    for k in range(TILES):
        r0, c0 = 16 * (k // 2), 128 * (k % 2)
        grad_o[r0:r0 + 16, c0:c0 + 128] = CD[k].astype(F32)
    gsum = jnp.sum(grad_o[...] * adv[...].astype(F32), axis=1, keepdims=True)
    ggain_o[...] = jnp.sum(e96 * gsum, axis=0, keepdims=True) / gainv[...].astype(F32)

    @pl.when(holder)
    def _():
        loop(NZ, lambda d: az(d).wait_send(), 1)

        def one(zz):
            p2, d = ad_of(zz)

            @pl.when(p2 != p)
            def _():
                d.wait_send()

        loop(NZ, one)

    @pl.when(active)
    def _():
        for d in range(1, NX):
            whole = AX.at[x]
            rcopy(whole, whole, sAX.at[d], rAX.at[x], xdev(lax.rem(x + d, NX))).wait_send()
        for k in range(TILES):
            @pl.when(jnp.logical_not(at_home & (p == k)))
            def _(k=k):
                cm(k).wait_send()

    for part, got, ys, out, ss, rs in ((ssp, ssr, ssy, rsv, sS, rS), (qp, qr, qy, wv, sQ, rQ)):
        pair_half(part, got, ss, rs).wait_send()
        for d in range(1, 8):
            y_send(ys, ss, rs, d).wait_send()
        pair_back(out, ss, rs).wait_send()

    for s in range(TILES // GROUP):
        for j in range(PER):
            xs, d = cx(j, s)

            @pl.when(xs != x)
            def _(d=d):
                d.wait_send()

    @pl.when(owner)
    def _():
        loop(NP, lambda d: cd(d).wait_send(), 1)


def per_device(x_slots, gain, adapter, readout, drift, ref_gap, rewards, groups, lengths, dest):
    V = pltpu.VMEM
    D = pltpu.SemaphoreType.DMA
    hbm_spec = pl.BlockSpec(memory_space=pltpu.HBM)
    vmem_spec = pl.BlockSpec(memory_space=pltpu.VMEM)
    chunks = V((NCH, 1, CHUNK), F32)
    half = V((HALF, 1, CHUNK), F32)
    along_y = V((8, HALF, 1, CHUNK), F32)
    grad, ggain = pl.pallas_call(
        kernel,
        out_shape=(
            jax.ShapeDtypeStruct((BLOCK, RANK), F32),
            jax.ShapeDtypeStruct((1, BLOCK), F32),
        ),
        in_specs=[hbm_spec] * 10,
        out_specs=(vmem_spec, vmem_spec),
        scratch_shapes=[
            V((FEAT, SLOTS), BF16), V((SLOTS, RANK), BF16), V((BLOCK, RANK), BF16), V((1, BLOCK), BF16),
            chunks, chunks, V((1, ROLLS), F32),
            V((1, ROLLS), jnp.int32), V((1, ROLLS), jnp.int32), V((1, ROLLS), jnp.int32),
            V((NCH, RANK, CHUNK), BF16), V((NCH, FEAT, CHUNK), BF16),
            V((NCH, RANK, CHUNK), BF16), V((FEAT, RANK), BF16), V((FEAT, CHUNK), F32),
            chunks, half, along_y, chunks, chunks, half, along_y, chunks, half, half, half,
            V((NZ, 16, 128), BF16), V((NX, TILES + 1, 16, 128), BF16),
            V((PER, TILES, 16, 128), BF16), V((NX, TILES, 16, 128), BF16),
            V((TILES, 16, 128), BF16), V((NZ, 16, 128), BF16), V((TILES, 16, 128), BF16),
            D((9,)), D((1,)),
            D((NZ,)), D((NZ,)), D((NZ,)), D((NP,)), D((NX,)), D((NX,)),
            D((10,)), D((10,)), D((10,)), D((10,)),
            D((PER, TILES // GROUP)), D((NX, TILES // GROUP)),
            D((TILES,)), D((NZ,)), D((NP,)), D((TILES,)),
        ],
        compiler_params=pltpu.CompilerParams(
            collective_id=0, has_side_effects=True, vmem_limit_bytes=60 * 1024 * 1024
        ),
    )(
        jnp.swapaxes(x_slots[0], 0, 1), gain.reshape(1, BLOCK), adapter, readout,
        drift.reshape(NCH, 1, CHUNK), ref_gap.reshape(NCH, 1, CHUNK), rewards, groups, lengths, dest,
    )
    return grad, ggain.reshape(BLOCK)


def solution(mesh):
    in_specs = (
        P("fsdp", None, "dp"),
        P("fsdp"),
        P("fsdp", None),
        P("fsdp", None, None),
        P("fsdp", None),
        P("fsdp", None),
        P("fsdp", None),
        P("fsdp", None),
        P("fsdp", None),
        P("fsdp", None),
    )
    out_specs = (P("fsdp", None), P("fsdp"))
    return jax.shard_map(
        per_device, mesh=mesh, in_specs=in_specs, out_specs=out_specs, check_vma=False
    )
```

```python
import math

import jax
import jax.numpy as jnp
from jax import lax
from jax.experimental import pallas as pl
from jax.experimental.pallas import tpu as pltpu
from jax.sharding import PartitionSpec as P

WIDTH = 4608
RANK = 256
SLOTS = 3072
LMAX = 64
ROLLS = 48
NP = 16
NZ = 12
NX = 4
FEAT = WIDTH // NP
BLOCK = WIDTH // (NZ * NX)
PER = FEAT // BLOCK
CHUNK = 256
NCH = SLOTS // CHUNK
TILES = 12
HALF = NCH // 2
GROUP = 4
FAR_Z = (6, 5, 7, 4, 8, 3, 9, 2, 10, 1, 11)
PIECES = ((0, 48), (48, 32), (80, 32))
NEAR_Z = (3, 9, 2, 10, 1, 11)
FAR_Y = (4, 3, 5, 2, 6, 1, 7)
FAR_P = (8, 7, 9, 6, 10, 5, 11, 4, 12, 3, 13, 2, 14, 1, 15)
kl_coef = 0.1
norm_eps = 1e-06
upper_log = math.log(1.2)
lower_log = math.log(0.8)
F32 = jnp.float32
BF16 = jnp.bfloat16
MESH = pl.DeviceIdType.MESH


def rcopy(src, dst, ssem, rsem, dev):
    return pltpu.make_async_remote_copy(
        src_ref=src, dst_ref=dst, send_sem=ssem, recv_sem=rsem, device_id=dev, device_id_type=MESH
    )


def loop(n, f, start=0):
    def step(i, carry):
        f(i)
        return carry

    lax.fori_loop(start, n, step, jnp.int32(0))


def eye(n, dtype=F32):
    r = lax.broadcasted_iota(jnp.int32, (n, n), 0)
    c = lax.broadcasted_iota(jnp.int32, (n, n), 1)
    return (r == c).astype(F32).astype(dtype)


def contract_last(a, b):
    return lax.dot_general(a, b, (((1,), (1,)), ((), ())), preferred_element_type=F32)


def kernel(
    x_h, gain_h, ad_h, ro_h, drift_h, gap_h, rew_h, grp_h, len_h, dst_h,
    tiles_o,
    xv, rv, adv, gainv, driftv, gapv, rewv, grpv, lenv, dstv,
    rT, zT, dT, W, gfull, gbuf,
    ssp, ssr, ssy, rsv, qp, qr, qy, wv, adv_s, inv_s, len_s,
    WX, CXs, CX, CZs, CM, CD,
    lsem, xsem,
    sAZ, rAZ, sAX, rAX,
    sS, rS, sQ, rQ,
    sCX, rCX, sCM, rCM, sCD, rCD,
):
    p = lax.axis_index("dp")
    c = lax.axis_index("fsdp")
    z = c // NX
    x = c % NX
    y = p // 2
    core = p % 2
    mine = core * HALF
    theirs = (1 - core) * HALF

    def zdev(z2):
        return (p, z2 * NX + x)

    def xdev(x2):
        return (p, z * NX + x2)

    def ddev(p2):
        return (p2, c)

    def act(x2):
        return lax.rem(x2 + p, 4) != 3

    sibling = (p + 1 - 2 * core, c)
    active = act(x)
    owner = p < TILES
    block = PER * p + jnp.minimum(lax.rem(x + p, 4), PER - 1)
    away = lax.rem(z - block // NX + NZ, NZ)

    small = [
        (ad_h, adv), (gain_h, gainv),
        (ro_h.at[0, pl.ds(theirs * CHUNK, SLOTS // 2)], rv.at[0:SLOTS // 2]),
        (ro_h.at[0, pl.ds(mine * CHUNK, SLOTS // 2)], rv.at[SLOTS // 2:SLOTS]),
        (rew_h, rewv), (grp_h, grpv), (len_h, lenv), (dst_h, dstv),
        (drift_h.at[pl.ds(mine, HALF)], driftv), (gap_h.at[pl.ds(mine, HALF)], gapv),
    ]
    loads = [pltpu.make_async_copy(s, d, lsem.at[i]) for i, (s, d) in enumerate(small)]
    xloads = [
        pltpu.make_async_copy(
            x_h.at[:, pl.ds(pl.multiple_of(first * CHUNK, SLOTS // 2), SLOTS // 2)],
            xv.at[:, i * (SLOTS // 2):(i + 1) * (SLOTS // 2)],
            xsem.at[i],
        )
        for i, first in enumerate((theirs, mine))
    ]
    loads[0].start()
    loads[1].start()
    for d in xloads:
        d.start()
    for d in loads[2:]:
        d.start()

    barrier = pltpu.get_barrier_semaphore()

    def greet(dev):
        pl.semaphore_signal(barrier, inc=1, device_id=dev, device_id_type=MESH)

    for d in FAR_Y:
        for k in range(2):
            greet(ddev(lax.rem(y + d, 8) * 2 + k))
    for d in NEAR_Z:
        greet(zdev(lax.rem(z + d, NZ)))
    for d in (2, 1, 3):
        greet(xdev(lax.rem(x + d, NX)))
    greet(sibling)
    loads[0].wait()
    loads[1].wait()

    @pl.when(active & (away == 0))
    def _():
        row = jnp.concatenate([gainv[...].astype(F32), jnp.ones((1, RANK - BLOCK), F32)], axis=1)
        WX[x, 0:16, :] = jnp.broadcast_to(row, (16, RANK)).astype(BF16)
        WX[x, 16:16 + BLOCK, :] = adv[...]

    pl.semaphore_wait(barrier, len(NEAR_Z) + NX + NP - 2)

    def az(d, s):
        part = WX.at[x, pl.ds(*PIECES[s])]
        return rcopy(part, part, sAZ.at[d, s], rAZ.at[s], zdev(lax.rem(z + d, NZ)))

    def az_all(dirs, s, act_on):
        for d in dirs:
            act_on(az(d, s))

    ROUTES = ((0, NEAR_Z), (3, (3, 2, 1)), (9, (11, 10)))

    @pl.when(active & (away == 0))
    def _():
        for s in range(len(PIECES)):
            az_all((3, 9), s, lambda d: d.start())
        for s in range(len(PIECES)):
            az_all((2, 10, 1, 11), s, lambda d: d.start())

    for d in xloads:
        d.wait()
    for i in range(NCH):
        xt = xv[:, i * CHUNK:(i + 1) * CHUNK].astype(F32)
        ssp[i] = jnp.sum(xt * xt, axis=0, keepdims=True)

    def pair(src, dst, ss, rs, i):
        return rcopy(src, dst, ss.at[i], rs.at[i], sibling)

    def pair_half(part, got, ss, rs):
        return pair(part.at[0:HALF], got, ss, rs, 8)

    def y_send(ys, ss, rs, d):
        return rcopy(ys.at[y], ys.at[y], ss.at[d], rs.at[y], ddev(lax.rem(y + d, 8) * 2 + core))

    def y_start(part, got, ys, ss, rs):
        pair_half(part, got, ss, rs).wait_recv()
        ys[y] = part[HALF:NCH] + got[...]
        for d in FAR_Y:
            y_send(ys, ss, rs, d).start()

    def y_sum(ys, ss, rs):
        for d in range(1, 8):
            y2 = lax.rem(y + d, 8)
            rcopy(ys.at[y2], ys.at[y2], ss.at[d], rs.at[y2], sibling).wait_recv()
        total = ys[0]
        for i in range(1, 8):
            total = total + ys[i]
        return total

    def pair_back(out, ss, rs):
        return pair(out.at[HALF:NCH], out.at[0:HALF], ss, rs, 9)

    pair_half(ssp, ssr, sS, rS).start()

    for d in loads[2:]:
        d.wait()
    ident = eye(RANK, BF16)
    for i in range(NCH):
        rT[i] = contract_last(ident, rv[i * CHUNK:(i + 1) * CHUNK, :]).astype(BF16)

    y_start(ssp, ssr, ssy, sS, rS)

    e48 = eye(ROLLS)

    def col(row):
        return jnp.sum(e48 * row, axis=1, keepdims=True)

    rew = rewv[...]
    grp = grpv[...].astype(F32)
    dst = dstv[...].astype(F32)
    ln = lenv[...].astype(F32)
    rew_c, len_c = col(rew), col(ln)
    same = (col(grp) == grp).astype(F32)
    members = jnp.sum(same, axis=0, keepdims=True)
    mean = jnp.sum(same * rew_c, axis=0, keepdims=True) / members
    var = jnp.sum(same * (rew_c - mean) ** 2, axis=0, keepdims=True) / members
    advantage = (rew - mean) / jnp.sqrt(jnp.maximum(var, 0.25))
    tokens = jnp.sum((col(dst) == dst).astype(F32) * len_c, axis=0, keepdims=True)
    adv_c, inv_c = col(advantage), col(1.0 / tokens)
    slot = lax.broadcasted_iota(jnp.int32, (ROLLS, CHUNK), 1)
    roll = lax.broadcasted_iota(jnp.int32, (ROLLS, CHUNK), 0)
    for i in range(HALF):
        pick = (roll == slot // LMAX + (mine + i) * (CHUNK // LMAX)).astype(F32)
        adv_s[i] = jnp.sum(pick * adv_c, axis=0, keepdims=True)
        inv_s[i] = jnp.sum(pick * inv_c, axis=0, keepdims=True)
        len_s[i] = jnp.sum(pick * len_c, axis=0, keepdims=True)

    def ax(d, s):
        part = WX.at[x, pl.ds(*PIECES[s])]
        return rcopy(part, part, sAX.at[d, s], rAX.at[x, s], xdev(lax.rem(x + d, NX)))

    @pl.when(active)
    def _():
        for s in range(len(PIECES)):
            part = WX.at[x, pl.ds(*PIECES[s])]

            @pl.when(away != 0)
            def _(part=part, s=s):
                rcopy(part, part, rAZ.at[s], rAZ.at[s], sibling).wait_recv()

            for place, dirs in ROUTES[1:]:
                @pl.when(away == place)
                def _(dirs=dirs, s=s):
                    az_all(dirs, s, lambda d: d.start())

            for d in (2, 1, 3):
                ax(d, s).start()

    total = y_sum(ssy, sS, rS)
    rsv[HALF:NCH] = lax.rsqrt(total * (1.0 / WIDTH) + norm_eps)
    pair_back(rsv, sS, rS).start()

    pair_back(rsv, sS, rS).wait_recv()
    for x2 in range(NX):
        @pl.when((x2 != x) & act(x2))
        def _(x2=x2):
            for s, piece in enumerate(PIECES):
                part = WX.at[x2, pl.ds(*piece)]
                rcopy(part, part, rAX.at[x2, s], rAX.at[x2, s], sibling).wait_recv()

    e96 = eye(BLOCK)
    for j in range(PER):
        xs = lax.rem(j + 3 * p, 4)
        W[BLOCK * j:BLOCK * j + BLOCK, :] = WX[xs, 16:16 + BLOCK, :]
        grow = WX[xs, 0:16, :].astype(F32)[0:1, 0:BLOCK]
        gfull[BLOCK * j:BLOCK * j + BLOCK, :] = jnp.broadcast_to(
            jnp.sum(e96 * grow, axis=1, keepdims=True), (BLOCK, CHUNK)
        )

    def qchunk(i):
        h = contract_last(W[...], rv[i * CHUNK:(i + 1) * CHUNK, :])
        xt = xv[:, i * CHUNK:(i + 1) * CHUNK].astype(F32)
        qp[i] = jnp.sum(xt * (h * gfull[...]), axis=0, keepdims=True) * rsv[i]

    def zchunk(i):
        xt = xv[:, i * CHUNK:(i + 1) * CHUNK].astype(F32)
        zT[i] = (xt * rsv[i] * gfull[...]).astype(BF16)

    for i in range(HALF):
        qchunk(i)
    pair_half(qp, qr, sQ, rQ).start()
    for i in range(HALF, NCH):
        qchunk(i)
    y_start(qp, qr, qy, sQ, rQ)
    for i in range(NCH):
        zchunk(i)
    shift = y_sum(qy, sQ, rQ)
    drift = driftv[...]
    gap = gapv[...]
    adv_rows = adv_s[...]
    logratio = drift + shift
    ratio = jnp.exp(logratio)
    keep = jnp.where(
        adv_rows >= 0,
        (drift <= jnp.float32(upper_log)).astype(F32),
        (drift >= jnp.float32(lower_log)).astype(F32),
    )
    dshift = inv_s[...] * (-adv_rows * ratio * keep + kl_coef * (1.0 - jnp.exp(gap - logratio)))
    place = lax.rem(lax.broadcasted_iota(jnp.int32, (HALF, 1, CHUNK), 2), LMAX).astype(F32)
    wv[HALF:NCH] = jnp.where(place < len_s[...], dshift, 0.0)
    pair_back(wv, sQ, rQ).start()

    def gsum(chunks):
        total = None
        for i in chunks:
            dT[i] = (rT[i].astype(F32) * wv[i]).astype(BF16)
            term = contract_last(zT[i], dT[i])
            total = term if total is None else total + term
        return total

    gbuf[...] = gsum(range(HALF, NCH))
    pair_back(wv, sQ, rQ).wait_recv()
    g = gsum(range(HALF)) + gbuf[...]
    for j in range(PER):
        for k in range(TILES):
            r0 = BLOCK * j + 16 * (k // 2)
            CXs[j, k] = g[r0:r0 + 16, 128 * (k % 2):128 * (k % 2) + 128].astype(BF16)

    def cx(j, s):
        xs = lax.rem(j + 3 * p, 4)
        part = pl.ds(GROUP * s, GROUP)
        return xs, rcopy(CXs.at[j, part], CX.at[x, part], sCX.at[j, s], rCX.at[x, s], xdev(xs))

    for s in range(TILES // GROUP):
        for j in range(PER):
            xs, d = cx(j, s)

            @pl.when(xs != x)
            def _(d=d):
                d.start()

    for j in range(PER):
        @pl.when(lax.rem(j + 3 * p, 4) == x)
        def _(j=j):
            CX[x] = CXs[j]

    at_home = block // NX == z

    def cm(k):
        return rcopy(CZs.at[k], CM.at[z], sCM.at[k], rCM.at[z], (k, block))

    @pl.when(active)
    def _():
        for s in range(TILES // GROUP):
            part = pl.ds(GROUP * s, GROUP)
            for d in (1, 3, 2):
                x2 = lax.rem(x + d, NX)
                rcopy(CX.at[x2, part], CX.at[x2, part], rCX.at[x2, s], rCX.at[x2, s], sibling).wait_recv()
            total = CX[0, part].astype(F32)
            for i in range(1, NX):
                total = total + CX[i, part].astype(F32)
            CZs[part] = total.astype(BF16)
            for k in range(GROUP * s, GROUP * s + GROUP):
                @pl.when(jnp.logical_not(at_home & (p == k)))
                def _(k=k):
                    cm(k).start()

                @pl.when(at_home & (p == k))
                def _(k=k):
                    CM[z] = CZs[k]

    feeder = c // PER

    def cd(d):
        return rcopy(CD.at[p], CD.at[p], sCD.at[d], rCD.at[p], ddev(lax.rem(p + d, NP)))

    @pl.when(owner)
    def _():
        for d in (0,) + FAR_Z[::-1]:
            zz = lax.rem(z + d, NZ)

            def arrive(zz=zz):
                rcopy(CM.at[zz], CM.at[zz], rCM.at[zz], rCM.at[zz], sibling).wait_recv()

            if d == 0:
                pl.when(feeder != p)(arrive)
            else:
                arrive()
        tile = CM[0].astype(F32)
        for i in range(1, NZ):
            tile = tile + CM[i].astype(F32)
        CD[p] = tile.astype(BF16)
        for d in FAR_P:
            cd(d).start()

    for k in range(TILES):
        @pl.when(p != k)
        def _(k=k):
            rcopy(CD.at[k], CD.at[k], rCD.at[k], rCD.at[k], sibling).wait_recv()
    tiles_o[...] = CD[...]

    @pl.when(active)
    def _():
        for s in range(len(PIECES)):
            for place, dirs in ROUTES:
                @pl.when(away == place)
                def _(dirs=dirs, s=s):
                    az_all(dirs, s, lambda d: d.wait_send())

            for d in (1, 2, 3):
                ax(d, s).wait_send()
        for k in range(TILES):
            @pl.when(jnp.logical_not(at_home & (p == k)))
            def _(k=k):
                cm(k).wait_send()

    for part, got, ys, out, ss, rs in ((ssp, ssr, ssy, rsv, sS, rS), (qp, qr, qy, wv, sQ, rQ)):
        pair_half(part, got, ss, rs).wait_send()
        for d in range(1, 8):
            y_send(ys, ss, rs, d).wait_send()
        pair_back(out, ss, rs).wait_send()

    for s in range(TILES // GROUP):
        for j in range(PER):
            xs, d = cx(j, s)

            @pl.when(xs != x)
            def _(d=d):
                d.wait_send()

    @pl.when(owner)
    def _():
        loop(NP, lambda d: cd(d).wait_send(), 1)


def finish(tiles, ad, gain, grad_o, ggain_o):
    for k in range(TILES):
        r0, c0 = 16 * (k // 2), 128 * (k % 2)
        grad_o[r0:r0 + 16, c0:c0 + 128] = tiles[k].astype(F32)
    gsum = jnp.sum(grad_o[...] * ad[...].astype(F32), axis=1, keepdims=True)
    ggain_o[...] = jnp.sum(eye(BLOCK) * gsum, axis=0, keepdims=True) / gain[...].astype(F32)


def per_device(x_slots, gain, adapter, readout, drift, ref_gap, rewards, groups, lengths, dest):
    V = pltpu.VMEM
    D = pltpu.SemaphoreType.DMA
    hbm_spec = pl.BlockSpec(memory_space=pltpu.HBM)
    vmem_spec = pl.BlockSpec(memory_space=pltpu.VMEM)
    chunks = V((NCH, 1, CHUNK), F32)
    half = V((HALF, 1, CHUNK), F32)
    along_y = V((8, HALF, 1, CHUNK), F32)
    tiles = pl.pallas_call(
        kernel,
        out_shape=jax.ShapeDtypeStruct((TILES, 16, 128), BF16),
        in_specs=[hbm_spec] * 10,
        out_specs=vmem_spec,
        scratch_shapes=[
            V((FEAT, SLOTS), BF16), V((SLOTS, RANK), BF16), V((BLOCK, RANK), BF16), V((1, BLOCK), BF16),
            half, half, V((1, ROLLS), F32),
            V((1, ROLLS), jnp.int32), V((1, ROLLS), jnp.int32), V((1, ROLLS), jnp.int32),
            V((NCH, RANK, CHUNK), BF16), V((NCH, FEAT, CHUNK), BF16),
            V((NCH, RANK, CHUNK), BF16), V((FEAT, RANK), BF16), V((FEAT, CHUNK), F32), V((FEAT, RANK), F32),
            chunks, half, along_y, chunks, chunks, half, along_y, chunks, half, half, half,
            V((NX, BLOCK + 16, RANK), BF16),
            V((PER, TILES, 16, 128), BF16), V((NX, TILES, 16, 128), BF16),
            V((TILES, 16, 128), BF16), V((NZ, 16, 128), BF16), V((TILES, 16, 128), BF16),
            D((10,)), D((2,)),
            D((NZ, len(PIECES))), D((len(PIECES),)), D((NX, len(PIECES))), D((NX, len(PIECES))),
            D((10,)), D((10,)), D((10,)), D((10,)),
            D((PER, TILES // GROUP)), D((NX, TILES // GROUP)),
            D((TILES,)), D((NZ,)), D((NP,)), D((TILES,)),
        ],
        compiler_params=pltpu.CompilerParams(
            collective_id=0, has_side_effects=True, vmem_limit_bytes=60 * 1024 * 1024
        ),
    )(
        jnp.swapaxes(x_slots[0], 0, 1), gain.reshape(1, BLOCK), adapter, readout,
        drift.reshape(NCH, 1, CHUNK), ref_gap.reshape(NCH, 1, CHUNK), rewards, groups, lengths, dest,
    )
    grad, ggain = pl.pallas_call(
        finish,
        out_shape=(
            jax.ShapeDtypeStruct((BLOCK, RANK), F32),
            jax.ShapeDtypeStruct((1, BLOCK), F32),
        ),
        in_specs=[vmem_spec] * 3,
        out_specs=(vmem_spec, vmem_spec),
    )(tiles, adapter, gain.reshape(1, BLOCK))
    return grad, ggain.reshape(BLOCK)


def solution(mesh):
    in_specs = (
        P("fsdp", None, "dp"),
        P("fsdp"),
        P("fsdp", None),
        P("fsdp", None, None),
        P("fsdp", None),
        P("fsdp", None),
        P("fsdp", None),
        P("fsdp", None),
        P("fsdp", None),
        P("fsdp", None),
    )
    out_specs = (P("fsdp", None), P("fsdp"))
    return jax.shard_map(
        per_device, mesh=mesh, in_specs=in_specs, out_specs=out_specs, check_vma=False
    )
```

```python
import math

import jax
import jax.numpy as jnp
from jax import lax
from jax.experimental import pallas as pl
from jax.experimental.pallas import tpu as pltpu
from jax.sharding import PartitionSpec as P

WIDTH = 4608
RANK = 256
SLOTS = 3072
LMAX = 64
ROLLS = 48
NP = 16
NZ = 12
NX = 4
FEAT = WIDTH // NP
BLOCK = WIDTH // (NZ * NX)
PER = FEAT // BLOCK
CHUNK = 256
NCH = SLOTS // CHUNK
TILES = 12
HALF = NCH // 2
GROUP = 4
FAR_Z = (6, 5, 7, 4, 8, 3, 9, 2, 10, 1, 11)
PIECES = ((0, 48), (48, 32), (80, 32))
NEAR_Z = (3, 9, 2, 10, 1, 11)
FAR_Y = (4, 3, 5, 2, 6, 1, 7)
FAR_P = (8, 7, 9, 6, 10, 5, 11, 4, 12, 3, 13, 2, 14, 1, 15)
kl_coef = 0.1
norm_eps = 1e-06
upper_log = math.log(1.2)
lower_log = math.log(0.8)
F32 = jnp.float32
BF16 = jnp.bfloat16
MESH = pl.DeviceIdType.MESH


def rcopy(src, dst, ssem, rsem, dev):
    return pltpu.make_async_remote_copy(
        src_ref=src, dst_ref=dst, send_sem=ssem, recv_sem=rsem, device_id=dev, device_id_type=MESH
    )


def loop(n, f, start=0):
    def step(i, carry):
        f(i)
        return carry

    lax.fori_loop(start, n, step, jnp.int32(0))


def eye(n, dtype=F32):
    r = lax.broadcasted_iota(jnp.int32, (n, n), 0)
    c = lax.broadcasted_iota(jnp.int32, (n, n), 1)
    return (r == c).astype(F32).astype(dtype)


def contract_last(a, b):
    return lax.dot_general(a, b, (((1,), (1,)), ((), ())), preferred_element_type=F32)


def kernel(
    x_h, gain_h, ad_h, ro_h, drift_h, gap_h, rew_h, grp_h, len_h, dst_h,
    tiles_o,
    xv, rv, adv, gainv, driftv, gapv, rewv, grpv, lenv, dstv,
    rT, zT, dT, W, gfull, gbuf,
    ssp, ssr, ssy, rsv, qp, qr, qy, wv, adv_s, inv_s, len_s,
    WX, CXs, CX, CZs, CM, CR, CD,
    lsem, xsem,
    sAZ, rAZ, sAX, rAX,
    sS, rS, sQ, rQ,
    sCX, rCX, sCM, rCM, sCR, rCR, sCD, rCD,
):
    p = lax.axis_index("dp")
    c = lax.axis_index("fsdp")
    z = c // NX
    x = c % NX
    y = p // 2
    core = p % 2
    mine = core * HALF
    theirs = (1 - core) * HALF

    def zdev(z2):
        return (p, z2 * NX + x)

    def xdev(x2):
        return (p, z * NX + x2)

    def ddev(p2):
        return (p2, c)

    def act(x2):
        return lax.rem(x2 + p, 4) != 3

    sibling = (p + 1 - 2 * core, c)
    active = act(x)
    owner = p < TILES
    block = PER * p + jnp.minimum(lax.rem(x + p, 4), PER - 1)
    away = lax.rem(z - block // NX + NZ, NZ)

    small = [
        (ad_h, adv), (gain_h, gainv),
        (ro_h.at[0, pl.ds(theirs * CHUNK, SLOTS // 2)], rv.at[0:SLOTS // 2]),
        (ro_h.at[0, pl.ds(mine * CHUNK, SLOTS // 2)], rv.at[SLOTS // 2:SLOTS]),
        (rew_h, rewv), (grp_h, grpv), (len_h, lenv), (dst_h, dstv),
        (drift_h.at[pl.ds(mine, HALF)], driftv), (gap_h.at[pl.ds(mine, HALF)], gapv),
    ]
    loads = [pltpu.make_async_copy(s, d, lsem.at[i]) for i, (s, d) in enumerate(small)]
    xloads = [
        pltpu.make_async_copy(
            x_h.at[:, pl.ds(pl.multiple_of(first * CHUNK, SLOTS // 2), SLOTS // 2)],
            xv.at[:, i * (SLOTS // 2):(i + 1) * (SLOTS // 2)],
            xsem.at[i],
        )
        for i, first in enumerate((theirs, mine))
    ]
    loads[0].start()
    loads[1].start()
    for d in xloads:
        d.start()
    for d in loads[2:]:
        d.start()

    barrier = pltpu.get_barrier_semaphore()

    def greet(dev):
        pl.semaphore_signal(barrier, inc=1, device_id=dev, device_id_type=MESH)

    for d in FAR_Y:
        for k in range(2):
            greet(ddev(lax.rem(y + d, 8) * 2 + k))
    for d in NEAR_Z:
        greet(zdev(lax.rem(z + d, NZ)))
    for d in (2, 1, 3):
        greet(xdev(lax.rem(x + d, NX)))
    greet(sibling)
    loads[0].wait()
    loads[1].wait()

    @pl.when(active & (away == 0))
    def _():
        row = jnp.concatenate([gainv[...].astype(F32), jnp.ones((1, RANK - BLOCK), F32)], axis=1)
        WX[x, 0:16, :] = jnp.broadcast_to(row, (16, RANK)).astype(BF16)
        WX[x, 16:16 + BLOCK, :] = adv[...]

    pl.semaphore_wait(barrier, len(NEAR_Z) + NX + NP - 2)

    def az(d, s):
        part = WX.at[x, pl.ds(*PIECES[s])]
        return rcopy(part, part, sAZ.at[d, s], rAZ.at[s], zdev(lax.rem(z + d, NZ)))

    def az_all(dirs, s, act_on):
        for d in dirs:
            act_on(az(d, s))

    ROUTES = ((0, NEAR_Z), (3, (3, 2, 1)), (9, (11, 10)))

    @pl.when(active & (away == 0))
    def _():
        for s in range(len(PIECES)):
            az_all((3, 9), s, lambda d: d.start())
        for s in range(len(PIECES)):
            az_all((2, 10, 1, 11), s, lambda d: d.start())

    for d in xloads:
        d.wait()
    for i in range(NCH):
        xt = xv[:, i * CHUNK:(i + 1) * CHUNK].astype(F32)
        ssp[i] = jnp.sum(xt * xt, axis=0, keepdims=True)

    def pair(src, dst, ss, rs, i):
        return rcopy(src, dst, ss.at[i], rs.at[i], sibling)

    def pair_half(part, got, ss, rs):
        return pair(part.at[0:HALF], got, ss, rs, 8)

    def y_send(ys, ss, rs, d):
        return rcopy(ys.at[y], ys.at[y], ss.at[d], rs.at[y], ddev(lax.rem(y + d, 8) * 2 + core))

    def y_start(part, got, ys, ss, rs):
        pair_half(part, got, ss, rs).wait_recv()
        ys[y] = part[HALF:NCH] + got[...]
        for d in FAR_Y:
            y_send(ys, ss, rs, d).start()

    def y_sum(ys, ss, rs):
        for d in range(1, 8):
            y2 = lax.rem(y + d, 8)
            rcopy(ys.at[y2], ys.at[y2], ss.at[d], rs.at[y2], sibling).wait_recv()
        total = ys[0]
        for i in range(1, 8):
            total = total + ys[i]
        return total

    def pair_back(out, ss, rs):
        return pair(out.at[HALF:NCH], out.at[0:HALF], ss, rs, 9)

    pair_half(ssp, ssr, sS, rS).start()

    for d in loads[2:]:
        d.wait()
    ident = eye(RANK, BF16)
    for i in range(NCH):
        rT[i] = contract_last(ident, rv[i * CHUNK:(i + 1) * CHUNK, :]).astype(BF16)

    y_start(ssp, ssr, ssy, sS, rS)

    e48 = eye(ROLLS)

    def col(row):
        return jnp.sum(e48 * row, axis=1, keepdims=True)

    rew = rewv[...]
    grp = grpv[...].astype(F32)
    dst = dstv[...].astype(F32)
    ln = lenv[...].astype(F32)
    rew_c, len_c = col(rew), col(ln)
    same = (col(grp) == grp).astype(F32)
    members = jnp.sum(same, axis=0, keepdims=True)
    mean = jnp.sum(same * rew_c, axis=0, keepdims=True) / members
    var = jnp.sum(same * (rew_c - mean) ** 2, axis=0, keepdims=True) / members
    advantage = (rew - mean) / jnp.sqrt(jnp.maximum(var, 0.25))
    tokens = jnp.sum((col(dst) == dst).astype(F32) * len_c, axis=0, keepdims=True)
    adv_c, inv_c = col(advantage), col(1.0 / tokens)
    slot = lax.broadcasted_iota(jnp.int32, (ROLLS, CHUNK), 1)
    roll = lax.broadcasted_iota(jnp.int32, (ROLLS, CHUNK), 0)
    for i in range(HALF):
        pick = (roll == slot // LMAX + (mine + i) * (CHUNK // LMAX)).astype(F32)
        adv_s[i] = jnp.sum(pick * adv_c, axis=0, keepdims=True)
        inv_s[i] = jnp.sum(pick * inv_c, axis=0, keepdims=True)
        len_s[i] = jnp.sum(pick * len_c, axis=0, keepdims=True)

    def ax(d, s):
        part = WX.at[x, pl.ds(*PIECES[s])]
        return rcopy(part, part, sAX.at[d, s], rAX.at[x, s], xdev(lax.rem(x + d, NX)))

    @pl.when(active)
    def _():
        for s in range(len(PIECES)):
            part = WX.at[x, pl.ds(*PIECES[s])]

            @pl.when(away != 0)
            def _(part=part, s=s):
                rcopy(part, part, rAZ.at[s], rAZ.at[s], sibling).wait_recv()

            for place, dirs in ROUTES[1:]:
                @pl.when(away == place)
                def _(dirs=dirs, s=s):
                    az_all(dirs, s, lambda d: d.start())

            for d in (2, 1, 3):
                ax(d, s).start()

    total = y_sum(ssy, sS, rS)
    rsv[HALF:NCH] = lax.rsqrt(total * (1.0 / WIDTH) + norm_eps)
    pair_back(rsv, sS, rS).start()

    pair_back(rsv, sS, rS).wait_recv()
    for x2 in range(NX):
        @pl.when((x2 != x) & act(x2))
        def _(x2=x2):
            for s, piece in enumerate(PIECES):
                part = WX.at[x2, pl.ds(*piece)]
                rcopy(part, part, rAX.at[x2, s], rAX.at[x2, s], sibling).wait_recv()

    e96 = eye(BLOCK)
    for j in range(PER):
        xs = lax.rem(j + 3 * p, 4)
        W[BLOCK * j:BLOCK * j + BLOCK, :] = WX[xs, 16:16 + BLOCK, :]
        grow = WX[xs, 0:16, :].astype(F32)[0:1, 0:BLOCK]
        gfull[BLOCK * j:BLOCK * j + BLOCK, :] = jnp.broadcast_to(
            jnp.sum(e96 * grow, axis=1, keepdims=True), (BLOCK, CHUNK)
        )

    def qchunk(i):
        h = contract_last(W[...], rv[i * CHUNK:(i + 1) * CHUNK, :])
        xt = xv[:, i * CHUNK:(i + 1) * CHUNK].astype(F32)
        zb = (xt * rsv[i] * gfull[...]).astype(BF16)
        zT[i] = zb
        qp[i] = jnp.sum(zb.astype(F32) * h, axis=0, keepdims=True)

    for i in range(HALF):
        qchunk(i)
    pair_half(qp, qr, sQ, rQ).start()
    for i in range(HALF, NCH):
        qchunk(i)
    y_start(qp, qr, qy, sQ, rQ)
    shift = y_sum(qy, sQ, rQ)
    drift = driftv[...]
    gap = gapv[...]
    adv_rows = adv_s[...]
    logratio = drift + shift
    ratio = jnp.exp(logratio)
    keep = jnp.where(
        adv_rows >= 0,
        (drift <= jnp.float32(upper_log)).astype(F32),
        (drift >= jnp.float32(lower_log)).astype(F32),
    )
    dshift = inv_s[...] * (-adv_rows * ratio * keep + kl_coef * (1.0 - jnp.exp(gap - logratio)))
    place = lax.rem(lax.broadcasted_iota(jnp.int32, (HALF, 1, CHUNK), 2), LMAX).astype(F32)
    wv[HALF:NCH] = jnp.where(place < len_s[...], dshift, 0.0)
    pair_back(wv, sQ, rQ).start()

    def gsum(chunks):
        total = None
        for i in chunks:
            dT[i] = (rT[i].astype(F32) * wv[i]).astype(BF16)
            term = contract_last(zT[i], dT[i])
            total = term if total is None else total + term
        return total

    gbuf[...] = gsum(range(HALF, NCH))
    pair_back(wv, sQ, rQ).wait_recv()
    g = gsum(range(HALF)) + gbuf[...]
    for j in range(PER):
        for k in range(TILES):
            r0 = BLOCK * j + 16 * (k // 2)
            CXs[j, k] = g[r0:r0 + 16, 128 * (k % 2):128 * (k % 2) + 128].astype(BF16)

    def cx(j, s):
        xs = lax.rem(j + 3 * p, 4)
        part = pl.ds(GROUP * s, GROUP)
        return xs, rcopy(CXs.at[j, part], CX.at[x, part], sCX.at[j, s], rCX.at[x, s], xdev(xs))

    for s in range(TILES // GROUP):
        for j in range(PER):
            xs, d = cx(j, s)

            @pl.when(xs != x)
            def _(d=d):
                d.start()

    for j in range(PER):
        @pl.when(lax.rem(j + 3 * p, 4) == x)
        def _(j=j):
            CX[x] = CXs[j]

    at_home = block // NX == z

    first_lines = block < NX

    def cr(s):
        part = pl.ds(GROUP * s, GROUP)
        return rcopy(CZs.at[part], CR.at[z, part], sCR.at[s], rCR.at[z, s], (p, block))

    def cm(k):
        return rcopy(CZs.at[k], CM.at[z], sCM.at[k], rCM.at[z], (k, block))

    @pl.when(active)
    def _():
        for s in range(TILES // GROUP):
            part = pl.ds(GROUP * s, GROUP)
            for d in (1, 3, 2):
                x2 = lax.rem(x + d, NX)
                rcopy(CX.at[x2, part], CX.at[x2, part], rCX.at[x2, s], rCX.at[x2, s], sibling).wait_recv()
            total = CX[0, part].astype(F32)
            for i in range(1, NX):
                total = total + CX[i, part].astype(F32)
            CZs[part] = total.astype(BF16)

            @pl.when(jnp.logical_not(first_lines))
            def _(s=s):
                for k in range(GROUP * s, GROUP * s + GROUP):
                    @pl.when(jnp.logical_not(at_home & (p == k)))
                    def _(k=k):
                        cm(k).start()

                    @pl.when(at_home & (p == k))
                    def _(k=k):
                        CM[z] = CZs[k]

            @pl.when(first_lines & jnp.logical_not(at_home))
            def _(s=s):
                cr(s).start()

            @pl.when(first_lines & at_home)
            def _(part=part):
                CR[z, part] = CZs[part]

    feeder = c // PER

    def cd(d):
        return rcopy(CD.at[p], CD.at[p], sCD.at[d], rCD.at[p], ddev(lax.rem(p + d, NP)))

    def spread_sib():
        return rcopy(CD, CD, sCD.at[0], rCD.at[0], sibling)

    def spread_y(d, k):
        return rcopy(CD, CD, sCD.at[2 * d + k], rCD.at[0], ddev(lax.rem(y + d, 8) * 2 + k))

    holds = feeder == p
    in_first = c < NX

    @pl.when(in_first & holds)
    def _():
        for s in range(TILES // GROUP):
            part = pl.ds(GROUP * s, GROUP)
            for d in FAR_Z[::-1]:
                zz = lax.rem(z + d, NZ)
                rcopy(CR.at[zz, part], CR.at[zz, part], rCR.at[zz, s], rCR.at[zz, s], sibling).wait_recv()
            total = CR[0, part].astype(F32)
            for i in range(1, NZ):
                total = total + CR[i, part].astype(F32)
            CD[part] = total.astype(BF16)
        spread_sib().start()
        for d in FAR_Y[::-1]:
            for k in range(2):
                spread_y(d, k).start()

    @pl.when(in_first & jnp.logical_not(holds))
    def _():
        rcopy(CD, CD, rCD.at[0], rCD.at[0], sibling).wait_recv()

    @pl.when(owner & jnp.logical_not(in_first))
    def _():
        for d in (0,) + FAR_Z[::-1]:
            zz = lax.rem(z + d, NZ)

            def arrive(zz=zz):
                rcopy(CM.at[zz], CM.at[zz], rCM.at[zz], rCM.at[zz], sibling).wait_recv()

            if d == 0:
                pl.when(feeder != p)(arrive)
            else:
                arrive()
        tile = CM[0].astype(F32)
        for i in range(1, NZ):
            tile = tile + CM[i].astype(F32)
        CD[p] = tile.astype(BF16)
        for d in FAR_P:
            cd(d).start()

    for k in range(TILES):
        @pl.when((p != k) & jnp.logical_not(in_first))
        def _(k=k):
            rcopy(CD.at[k], CD.at[k], rCD.at[k], rCD.at[k], sibling).wait_recv()
    tiles_o[...] = CD[...]

    @pl.when(active)
    def _():
        for s in range(len(PIECES)):
            for place, dirs in ROUTES:
                @pl.when(away == place)
                def _(dirs=dirs, s=s):
                    az_all(dirs, s, lambda d: d.wait_send())

            for d in (1, 2, 3):
                ax(d, s).wait_send()
        for k in range(TILES):
            @pl.when(jnp.logical_not(first_lines | (at_home & (p == k))))
            def _(k=k):
                cm(k).wait_send()
        for s in range(TILES // GROUP):
            @pl.when(first_lines & jnp.logical_not(at_home))
            def _(s=s):
                cr(s).wait_send()

    for part, got, ys, out, ss, rs in ((ssp, ssr, ssy, rsv, sS, rS), (qp, qr, qy, wv, sQ, rQ)):
        pair_half(part, got, ss, rs).wait_send()
        for d in range(1, 8):
            y_send(ys, ss, rs, d).wait_send()
        pair_back(out, ss, rs).wait_send()

    for s in range(TILES // GROUP):
        for j in range(PER):
            xs, d = cx(j, s)

            @pl.when(xs != x)
            def _(d=d):
                d.wait_send()

    @pl.when(owner & jnp.logical_not(in_first))
    def _():
        loop(NP, lambda d: cd(d).wait_send(), 1)

    @pl.when(in_first & holds)
    def _():
        spread_sib().wait_send()
        for d in FAR_Y:
            for k in range(2):
                spread_y(d, k).wait_send()


def finish(tiles, ad, gain, grad_o, ggain_o):
    for k in range(TILES):
        r0, c0 = 16 * (k // 2), 128 * (k % 2)
        grad_o[r0:r0 + 16, c0:c0 + 128] = tiles[k].astype(F32)
    gsum = jnp.sum(grad_o[...] * ad[...].astype(F32), axis=1, keepdims=True)
    ggain_o[...] = jnp.sum(eye(BLOCK) * gsum, axis=0, keepdims=True) / gain[...].astype(F32)


def per_device(x_slots, gain, adapter, readout, drift, ref_gap, rewards, groups, lengths, dest):
    V = pltpu.VMEM
    D = pltpu.SemaphoreType.DMA
    hbm_spec = pl.BlockSpec(memory_space=pltpu.HBM)
    vmem_spec = pl.BlockSpec(memory_space=pltpu.VMEM)
    chunks = V((NCH, 1, CHUNK), F32)
    half = V((HALF, 1, CHUNK), F32)
    along_y = V((8, HALF, 1, CHUNK), F32)
    tiles = pl.pallas_call(
        kernel,
        out_shape=jax.ShapeDtypeStruct((TILES, 16, 128), BF16),
        in_specs=[hbm_spec] * 10,
        out_specs=vmem_spec,
        scratch_shapes=[
            V((FEAT, SLOTS), BF16), V((SLOTS, RANK), BF16), V((BLOCK, RANK), BF16), V((1, BLOCK), BF16),
            half, half, V((1, ROLLS), F32),
            V((1, ROLLS), jnp.int32), V((1, ROLLS), jnp.int32), V((1, ROLLS), jnp.int32),
            V((NCH, RANK, CHUNK), BF16), V((NCH, FEAT, CHUNK), BF16),
            V((NCH, RANK, CHUNK), BF16), V((FEAT, RANK), BF16), V((FEAT, CHUNK), F32), V((FEAT, RANK), F32),
            chunks, half, along_y, chunks, chunks, half, along_y, chunks, half, half, half,
            V((NX, BLOCK + 16, RANK), BF16),
            V((PER, TILES, 16, 128), BF16), V((NX, TILES, 16, 128), BF16),
            V((TILES, 16, 128), BF16), V((NZ, 16, 128), BF16), V((NZ, TILES, 16, 128), BF16),
            V((TILES, 16, 128), BF16),
            D((10,)), D((2,)),
            D((NZ, len(PIECES))), D((len(PIECES),)), D((NX, len(PIECES))), D((NX, len(PIECES))),
            D((10,)), D((10,)), D((10,)), D((10,)),
            D((PER, TILES // GROUP)), D((NX, TILES // GROUP)),
            D((TILES,)), D((NZ,)), D((TILES // GROUP,)), D((NZ, TILES // GROUP)), D((NP,)), D((TILES,)),
        ],
        compiler_params=pltpu.CompilerParams(
            collective_id=0, has_side_effects=True, vmem_limit_bytes=60 * 1024 * 1024
        ),
    )(
        jnp.swapaxes(x_slots[0], 0, 1), gain.reshape(1, BLOCK), adapter, readout,
        drift.reshape(NCH, 1, CHUNK), ref_gap.reshape(NCH, 1, CHUNK), rewards, groups, lengths, dest,
    )
    grad, ggain = pl.pallas_call(
        finish,
        out_shape=(
            jax.ShapeDtypeStruct((BLOCK, RANK), F32),
            jax.ShapeDtypeStruct((1, BLOCK), F32),
        ),
        in_specs=[vmem_spec] * 3,
        out_specs=(vmem_spec, vmem_spec),
    )(tiles, adapter, gain.reshape(1, BLOCK))
    return grad, ggain.reshape(BLOCK)


def solution(mesh):
    in_specs = (
        P("fsdp", None, "dp"),
        P("fsdp"),
        P("fsdp", None),
        P("fsdp", None, None),
        P("fsdp", None),
        P("fsdp", None),
        P("fsdp", None),
        P("fsdp", None),
        P("fsdp", None),
        P("fsdp", None),
    )
    out_specs = (P("fsdp", None), P("fsdp"))
    return jax.shard_map(
        per_device, mesh=mesh, in_specs=in_specs, out_specs=out_specs, check_vma=False
    )
```

```python
import math

import jax
import jax.numpy as jnp
from jax import lax
from jax.experimental import pallas as pl
from jax.experimental.pallas import tpu as pltpu
from jax.sharding import PartitionSpec as P

WIDTH = 4608
RANK = 256
SLOTS = 3072
LMAX = 64
ROLLS = 48
NP = 16
NZ = 12
NX = 4
FEAT = WIDTH // NP
BLOCK = WIDTH // (NZ * NX)
PER = FEAT // BLOCK
CHUNK = 256
NCH = SLOTS // CHUNK
TILES = 12
HALF = NCH // 2
GROUP = 4
FIRST = 12
FAR_Z = (6, 5, 7, 4, 8, 3, 9, 2, 10, 1, 11)
PIECES = ((0, 48), (48, 32), (80, 32))
NEAR_Z = (3, 9, 2, 10, 1, 11)
FAR_Y = (4, 3, 5, 2, 6, 1, 7)
FAR_P = (8, 7, 9, 6, 10, 5, 11, 4, 12, 3, 13, 2, 14, 1, 15)
kl_coef = 0.1
norm_eps = 1e-06
upper_log = math.log(1.2)
lower_log = math.log(0.8)
F32 = jnp.float32
BF16 = jnp.bfloat16
MESH = pl.DeviceIdType.MESH


def rcopy(src, dst, ssem, rsem, dev):
    return pltpu.make_async_remote_copy(
        src_ref=src, dst_ref=dst, send_sem=ssem, recv_sem=rsem, device_id=dev, device_id_type=MESH
    )


def loop(n, f, start=0):
    def step(i, carry):
        f(i)
        return carry

    lax.fori_loop(start, n, step, jnp.int32(0))


def eye(n, dtype=F32):
    r = lax.broadcasted_iota(jnp.int32, (n, n), 0)
    c = lax.broadcasted_iota(jnp.int32, (n, n), 1)
    return (r == c).astype(F32).astype(dtype)


def contract_last(a, b):
    return lax.dot_general(a, b, (((1,), (1,)), ((), ())), preferred_element_type=F32)


def kernel(
    x_h, gain_h, ad_h, ro_h, drift_h, gap_h, rew_h, grp_h, len_h, dst_h,
    tiles_o,
    xv, rv, adv, gainv, driftv, gapv, rewv, grpv, lenv, dstv,
    rT, zT, dT, W, gfull, gbuf,
    ssp, ssr, ssy, rsv, qp, qr, qy, wv, adv_s, inv_s, len_s,
    WX, CXs, CX, CZs, CM, CN, CD,
    lsem, xsem,
    sAZ, rAZ, sAX, rAX,
    sS, rS, sQ, rQ,
    sCX, rCX, sCM, rCM, sCN, rCN, rCN2, sCD, rCD,
):
    p = lax.axis_index("dp")
    c = lax.axis_index("fsdp")
    z = c // NX
    x = c % NX
    y = p // 2
    core = p % 2
    mine = core * HALF
    theirs = (1 - core) * HALF

    def zdev(z2):
        return (p, z2 * NX + x)

    def xdev(x2):
        return (p, z * NX + x2)

    def ddev(p2):
        return (p2, c)

    def act(x2):
        return lax.rem(x2 + p, 4) != 3

    sibling = (p + 1 - 2 * core, c)
    active = act(x)
    owner = p < TILES
    block = PER * p + jnp.minimum(lax.rem(x + p, 4), PER - 1)
    away = lax.rem(z - block // NX + NZ, NZ)

    small = [
        (ad_h, adv), (gain_h, gainv),
        (ro_h.at[0, pl.ds(theirs * CHUNK, SLOTS // 2)], rv.at[0:SLOTS // 2]),
        (ro_h.at[0, pl.ds(mine * CHUNK, SLOTS // 2)], rv.at[SLOTS // 2:SLOTS]),
        (rew_h, rewv), (grp_h, grpv), (len_h, lenv), (dst_h, dstv),
        (drift_h.at[pl.ds(mine, HALF)], driftv), (gap_h.at[pl.ds(mine, HALF)], gapv),
    ]
    loads = [pltpu.make_async_copy(s, d, lsem.at[i]) for i, (s, d) in enumerate(small)]
    xloads = [
        pltpu.make_async_copy(
            x_h.at[:, pl.ds(pl.multiple_of(first * CHUNK, SLOTS // 2), SLOTS // 2)],
            xv.at[:, i * (SLOTS // 2):(i + 1) * (SLOTS // 2)],
            xsem.at[i],
        )
        for i, first in enumerate((theirs, mine))
    ]
    loads[0].start()
    loads[1].start()
    for d in xloads:
        d.start()
    for d in loads[2:]:
        d.start()

    barrier = pltpu.get_barrier_semaphore()

    def greet(dev):
        pl.semaphore_signal(barrier, inc=1, device_id=dev, device_id_type=MESH)

    for d in FAR_Y:
        for k in range(2):
            greet(ddev(lax.rem(y + d, 8) * 2 + k))
    for d in NEAR_Z:
        greet(zdev(lax.rem(z + d, NZ)))
    for d in (2, 1, 3):
        greet(xdev(lax.rem(x + d, NX)))
    greet(sibling)
    loads[0].wait()
    loads[1].wait()

    @pl.when(active & (away == 0))
    def _():
        row = jnp.concatenate([gainv[...].astype(F32), jnp.ones((1, RANK - BLOCK), F32)], axis=1)
        WX[x, 0:16, :] = jnp.broadcast_to(row, (16, RANK)).astype(BF16)
        WX[x, 16:16 + BLOCK, :] = adv[...]

    pl.semaphore_wait(barrier, len(NEAR_Z) + NX + NP - 2)

    def az(d, s):
        part = WX.at[x, pl.ds(*PIECES[s])]
        return rcopy(part, part, sAZ.at[d, s], rAZ.at[s], zdev(lax.rem(z + d, NZ)))

    def az_all(dirs, s, act_on):
        for d in dirs:
            act_on(az(d, s))

    ROUTES = ((0, NEAR_Z), (3, (3, 2, 1)), (9, (11, 10)))

    @pl.when(active & (away == 0))
    def _():
        for s in range(len(PIECES)):
            az_all((3, 9), s, lambda d: d.start())
        for s in range(len(PIECES)):
            az_all((2, 10, 1, 11), s, lambda d: d.start())

    for d in xloads:
        d.wait()
    for i in range(NCH):
        xt = xv[:, i * CHUNK:(i + 1) * CHUNK].astype(F32)
        ssp[i] = jnp.sum(xt * xt, axis=0, keepdims=True)

    def pair(src, dst, ss, rs, i):
        return rcopy(src, dst, ss.at[i], rs.at[i], sibling)

    def pair_half(part, got, ss, rs):
        return pair(part.at[0:HALF], got, ss, rs, 8)

    def y_send(ys, ss, rs, d):
        return rcopy(ys.at[y], ys.at[y], ss.at[d], rs.at[y], ddev(lax.rem(y + d, 8) * 2 + core))

    def y_start(part, got, ys, ss, rs):
        pair_half(part, got, ss, rs).wait_recv()
        ys[y] = part[HALF:NCH] + got[...]
        for d in FAR_Y:
            y_send(ys, ss, rs, d).start()

    def y_sum(ys, ss, rs):
        for d in range(1, 8):
            y2 = lax.rem(y + d, 8)
            rcopy(ys.at[y2], ys.at[y2], ss.at[d], rs.at[y2], sibling).wait_recv()
        total = ys[0]
        for i in range(1, 8):
            total = total + ys[i]
        return total

    def pair_back(out, ss, rs):
        return pair(out.at[HALF:NCH], out.at[0:HALF], ss, rs, 9)

    pair_half(ssp, ssr, sS, rS).start()

    for d in loads[2:]:
        d.wait()
    ident = eye(RANK, BF16)
    for i in range(NCH):
        rT[i] = contract_last(ident, rv[i * CHUNK:(i + 1) * CHUNK, :]).astype(BF16)

    y_start(ssp, ssr, ssy, sS, rS)

    e48 = eye(ROLLS)

    def col(row):
        return jnp.sum(e48 * row, axis=1, keepdims=True)

    rew = rewv[...]
    grp = grpv[...].astype(F32)
    dst = dstv[...].astype(F32)
    ln = lenv[...].astype(F32)
    rew_c, len_c = col(rew), col(ln)
    same = (col(grp) == grp).astype(F32)
    members = jnp.sum(same, axis=0, keepdims=True)
    mean = jnp.sum(same * rew_c, axis=0, keepdims=True) / members
    var = jnp.sum(same * (rew_c - mean) ** 2, axis=0, keepdims=True) / members
    advantage = (rew - mean) / jnp.sqrt(jnp.maximum(var, 0.25))
    tokens = jnp.sum((col(dst) == dst).astype(F32) * len_c, axis=0, keepdims=True)
    adv_c, inv_c = col(advantage), col(1.0 / tokens)
    slot = lax.broadcasted_iota(jnp.int32, (ROLLS, CHUNK), 1)
    roll = lax.broadcasted_iota(jnp.int32, (ROLLS, CHUNK), 0)
    for i in range(HALF):
        pick = (roll == slot // LMAX + (mine + i) * (CHUNK // LMAX)).astype(F32)
        adv_s[i] = jnp.sum(pick * adv_c, axis=0, keepdims=True)
        inv_s[i] = jnp.sum(pick * inv_c, axis=0, keepdims=True)
        len_s[i] = jnp.sum(pick * len_c, axis=0, keepdims=True)

    def ax(d, s):
        part = WX.at[x, pl.ds(*PIECES[s])]
        return rcopy(part, part, sAX.at[d, s], rAX.at[x, s], xdev(lax.rem(x + d, NX)))

    @pl.when(active)
    def _():
        for s in range(len(PIECES)):
            part = WX.at[x, pl.ds(*PIECES[s])]

            @pl.when(away != 0)
            def _(part=part, s=s):
                rcopy(part, part, rAZ.at[s], rAZ.at[s], sibling).wait_recv()

            for place, dirs in ROUTES[1:]:
                @pl.when(away == place)
                def _(dirs=dirs, s=s):
                    az_all(dirs, s, lambda d: d.start())

            for d in (2, 1, 3):
                ax(d, s).start()

    total = y_sum(ssy, sS, rS)
    rsv[HALF:NCH] = lax.rsqrt(total * (1.0 / WIDTH) + norm_eps)
    pair_back(rsv, sS, rS).start()

    pair_back(rsv, sS, rS).wait_recv()
    for x2 in range(NX):
        @pl.when((x2 != x) & act(x2))
        def _(x2=x2):
            for s, piece in enumerate(PIECES):
                part = WX.at[x2, pl.ds(*piece)]
                rcopy(part, part, rAX.at[x2, s], rAX.at[x2, s], sibling).wait_recv()

    e96 = eye(BLOCK)
    for j in range(PER):
        xs = lax.rem(j + 3 * p, 4)
        W[BLOCK * j:BLOCK * j + BLOCK, :] = WX[xs, 16:16 + BLOCK, :]
        grow = WX[xs, 0:16, :].astype(F32)[0:1, 0:BLOCK]
        gfull[BLOCK * j:BLOCK * j + BLOCK, :] = jnp.broadcast_to(
            jnp.sum(e96 * grow, axis=1, keepdims=True), (BLOCK, CHUNK)
        )

    def qchunk(i):
        h = contract_last(W[...], rv[i * CHUNK:(i + 1) * CHUNK, :])
        xt = xv[:, i * CHUNK:(i + 1) * CHUNK].astype(F32)
        zb = (xt * rsv[i] * gfull[...]).astype(BF16)
        zT[i] = zb
        qp[i] = jnp.sum(zb.astype(F32) * h, axis=0, keepdims=True)

    for i in range(HALF):
        qchunk(i)
    pair_half(qp, qr, sQ, rQ).start()
    for i in range(HALF, NCH):
        qchunk(i)
    y_start(qp, qr, qy, sQ, rQ)
    shift = y_sum(qy, sQ, rQ)
    drift = driftv[...]
    gap = gapv[...]
    adv_rows = adv_s[...]
    logratio = drift + shift
    ratio = jnp.exp(logratio)
    keep = jnp.where(
        adv_rows >= 0,
        (drift <= jnp.float32(upper_log)).astype(F32),
        (drift >= jnp.float32(lower_log)).astype(F32),
    )
    dshift = inv_s[...] * (-adv_rows * ratio * keep + kl_coef * (1.0 - jnp.exp(gap - logratio)))
    place = lax.rem(lax.broadcasted_iota(jnp.int32, (HALF, 1, CHUNK), 2), LMAX).astype(F32)
    wv[HALF:NCH] = jnp.where(place < len_s[...], dshift, 0.0)
    pair_back(wv, sQ, rQ).start()

    def gsum(chunks):
        total = None
        for i in chunks:
            dT[i] = (rT[i].astype(F32) * wv[i]).astype(BF16)
            term = contract_last(zT[i], dT[i])
            total = term if total is None else total + term
        return total

    gbuf[...] = gsum(range(HALF, NCH))
    pair_back(wv, sQ, rQ).wait_recv()
    g = gsum(range(HALF)) + gbuf[...]
    for j in range(PER):
        for k in range(TILES):
            r0 = BLOCK * j + 16 * (k // 2)
            CXs[j, k] = g[r0:r0 + 16, 128 * (k % 2):128 * (k % 2) + 128].astype(BF16)

    def cx(j, s):
        xs = lax.rem(j + 3 * p, 4)
        part = pl.ds(GROUP * s, GROUP)
        return xs, rcopy(CXs.at[j, part], CX.at[x, part], sCX.at[j, s], rCX.at[x, s], xdev(xs))

    for s in range(TILES // GROUP):
        for j in range(PER):
            xs, d = cx(j, s)

            @pl.when(xs != x)
            def _(d=d):
                d.start()

    for j in range(PER):
        @pl.when(lax.rem(j + 3 * p, 4) == x)
        def _(j=j):
            CX[x] = CXs[j]

    at_home = block // NX == z

    first_lines = block < FIRST

    def near_owner(plane, m):
        return lax.rem(plane // 2 + 7 + m // 2, 8) * 2 + m % 2

    def cn(m):
        return rcopy(CZs.at[pl.ds(2 * m, 2)], CN.at[z], sCN.at[m], rCN.at[z], (near_owner(p, m), block))


    def cm(k):
        return rcopy(CZs.at[k], CM.at[z], sCM.at[k], rCM.at[z], (k, block))

    @pl.when(active)
    def _():
        for s in range(TILES // GROUP):
            part = pl.ds(GROUP * s, GROUP)
            for d in (1, 3, 2):
                x2 = lax.rem(x + d, NX)
                rcopy(CX.at[x2, part], CX.at[x2, part], rCX.at[x2, s], rCX.at[x2, s], sibling).wait_recv()
            total = CX[0, part].astype(F32)
            for i in range(1, NX):
                total = total + CX[i, part].astype(F32)
            CZs[part] = total.astype(BF16)

            @pl.when(first_lines)
            def _(s=s):
                for m in range(GROUP * s // 2, GROUP * s // 2 + GROUP // 2):
                    @pl.when(jnp.logical_not(at_home & (p == near_owner(p, m))))
                    def _(m=m):
                        cn(m).start()

                    @pl.when(at_home & (p == near_owner(p, m)))
                    def _(m=m):
                        CN[z] = CZs[2 * m:2 * m + 2]

            @pl.when(block >= FIRST)
            def _(s=s):
                for k in range(GROUP * s, GROUP * s + GROUP):
                    @pl.when(jnp.logical_not(at_home & (p == k)))
                    def _(k=k):
                        cm(k).start()

                    @pl.when(at_home & (p == k))
                    def _(k=k):
                        CM[z] = CZs[k]

    feeder = c // PER

    def cd(d):
        return rcopy(CD.at[p], CD.at[p], sCD.at[d], rCD.at[p], ddev(lax.rem(p + d, NP)))

    in_first = c < FIRST
    others = c >= FIRST

    def cdn(m, d):
        part = CD.at[pl.ds(2 * m, 2)]
        return rcopy(part, part, sCD.at[d], rCN2.at[m], ddev(lax.rem(p + d, NP)))

    for m in range(6):
        @pl.when(in_first & (p == near_owner(feeder, m)))
        def _(m=m):
            for d in (0,) + FAR_Z[::-1]:
                zz = lax.rem(z + d, NZ)

                def arrive(zz=zz):
                    rcopy(CN.at[zz], CN.at[zz], rCN.at[zz], rCN.at[zz], sibling).wait_recv()

                if d == 0:
                    pl.when(feeder != p)(arrive)
                else:
                    arrive()
            total = CN[0].astype(F32)
            for i in range(1, NZ):
                total = total + CN[i].astype(F32)
            CD[2 * m:2 * m + 2] = total.astype(BF16)
            for d in FAR_P[::-1]:
                cdn(m, d).start()

    for m in range(6):
        @pl.when(in_first & (p != near_owner(feeder, m)))
        def _(m=m):
            part = CD.at[pl.ds(2 * m, 2)]
            rcopy(part, part, rCN2.at[m], rCN2.at[m], sibling).wait_recv()

    @pl.when(owner & others)
    def _():
        for d in (0,) + FAR_Z[::-1]:
            zz = lax.rem(z + d, NZ)

            def arrive(zz=zz):
                rcopy(CM.at[zz], CM.at[zz], rCM.at[zz], rCM.at[zz], sibling).wait_recv()

            if d == 0:
                pl.when(feeder != p)(arrive)
            else:
                arrive()
        tile = CM[0].astype(F32)
        for i in range(1, NZ):
            tile = tile + CM[i].astype(F32)
        CD[p] = tile.astype(BF16)
        for d in FAR_P:
            cd(d).start()

    for k in range(TILES):
        @pl.when((p != k) & others)
        def _(k=k):
            rcopy(CD.at[k], CD.at[k], rCD.at[k], rCD.at[k], sibling).wait_recv()
    tiles_o[...] = CD[...]

    @pl.when(active)
    def _():
        for s in range(len(PIECES)):
            for place, dirs in ROUTES:
                @pl.when(away == place)
                def _(dirs=dirs, s=s):
                    az_all(dirs, s, lambda d: d.wait_send())

            for d in (1, 2, 3):
                ax(d, s).wait_send()
        for k in range(TILES):
            @pl.when((block >= FIRST) & jnp.logical_not(at_home & (p == k)))
            def _(k=k):
                cm(k).wait_send()
        for m in range(6):
            @pl.when(first_lines & jnp.logical_not(at_home & (p == near_owner(p, m))))
            def _(m=m):
                cn(m).wait_send()

    for part, got, ys, out, ss, rs in ((ssp, ssr, ssy, rsv, sS, rS), (qp, qr, qy, wv, sQ, rQ)):
        pair_half(part, got, ss, rs).wait_send()
        for d in range(1, 8):
            y_send(ys, ss, rs, d).wait_send()
        pair_back(out, ss, rs).wait_send()

    for s in range(TILES // GROUP):
        for j in range(PER):
            xs, d = cx(j, s)

            @pl.when(xs != x)
            def _(d=d):
                d.wait_send()

    @pl.when(owner & others)
    def _():
        loop(NP, lambda d: cd(d).wait_send(), 1)

    for m in range(6):
        @pl.when(in_first & (p == near_owner(feeder, m)))
        def _(m=m):
            for d in FAR_P:
                cdn(m, d).wait_send()


def finish(tiles, ad, gain, grad_o, ggain_o):
    for k in range(TILES):
        r0, c0 = 16 * (k // 2), 128 * (k % 2)
        grad_o[r0:r0 + 16, c0:c0 + 128] = tiles[k].astype(F32)
    gsum = jnp.sum(grad_o[...] * ad[...].astype(F32), axis=1, keepdims=True)
    ggain_o[...] = jnp.sum(eye(BLOCK) * gsum, axis=0, keepdims=True) / gain[...].astype(F32)


def per_device(x_slots, gain, adapter, readout, drift, ref_gap, rewards, groups, lengths, dest):
    V = pltpu.VMEM
    D = pltpu.SemaphoreType.DMA
    hbm_spec = pl.BlockSpec(memory_space=pltpu.HBM)
    vmem_spec = pl.BlockSpec(memory_space=pltpu.VMEM)
    chunks = V((NCH, 1, CHUNK), F32)
    half = V((HALF, 1, CHUNK), F32)
    along_y = V((8, HALF, 1, CHUNK), F32)
    tiles = pl.pallas_call(
        kernel,
        out_shape=jax.ShapeDtypeStruct((TILES, 16, 128), BF16),
        in_specs=[hbm_spec] * 10,
        out_specs=vmem_spec,
        scratch_shapes=[
            V((FEAT, SLOTS), BF16), V((SLOTS, RANK), BF16), V((BLOCK, RANK), BF16), V((1, BLOCK), BF16),
            half, half, V((1, ROLLS), F32),
            V((1, ROLLS), jnp.int32), V((1, ROLLS), jnp.int32), V((1, ROLLS), jnp.int32),
            V((NCH, RANK, CHUNK), BF16), V((NCH, FEAT, CHUNK), BF16),
            V((NCH, RANK, CHUNK), BF16), V((FEAT, RANK), BF16), V((FEAT, CHUNK), F32), V((FEAT, RANK), F32),
            chunks, half, along_y, chunks, chunks, half, along_y, chunks, half, half, half,
            V((NX, BLOCK + 16, RANK), BF16),
            V((PER, TILES, 16, 128), BF16), V((NX, TILES, 16, 128), BF16),
            V((TILES, 16, 128), BF16), V((NZ, 16, 128), BF16),
            V((NZ, 2, 16, 128), BF16), V((TILES, 16, 128), BF16),
            D((10,)), D((2,)),
            D((NZ, len(PIECES))), D((len(PIECES),)), D((NX, len(PIECES))), D((NX, len(PIECES))),
            D((10,)), D((10,)), D((10,)), D((10,)),
            D((PER, TILES // GROUP)), D((NX, TILES // GROUP)),
            D((TILES,)), D((NZ,)), D((6,)), D((NZ,)), D((6,)), D((NP,)), D((TILES,)),
        ],
        compiler_params=pltpu.CompilerParams(
            collective_id=0, has_side_effects=True, vmem_limit_bytes=60 * 1024 * 1024
        ),
    )(
        jnp.swapaxes(x_slots[0], 0, 1), gain.reshape(1, BLOCK), adapter, readout,
        drift.reshape(NCH, 1, CHUNK), ref_gap.reshape(NCH, 1, CHUNK), rewards, groups, lengths, dest,
    )
    grad, ggain = pl.pallas_call(
        finish,
        out_shape=(
            jax.ShapeDtypeStruct((BLOCK, RANK), F32),
            jax.ShapeDtypeStruct((1, BLOCK), F32),
        ),
        in_specs=[vmem_spec] * 3,
        out_specs=(vmem_spec, vmem_spec),
    )(tiles, adapter, gain.reshape(1, BLOCK))
    return grad, ggain.reshape(BLOCK)


def solution(mesh):
    in_specs = (
        P("fsdp", None, "dp"),
        P("fsdp"),
        P("fsdp", None),
        P("fsdp", None, None),
        P("fsdp", None),
        P("fsdp", None),
        P("fsdp", None),
        P("fsdp", None),
        P("fsdp", None),
        P("fsdp", None),
    )
    out_specs = (P("fsdp", None), P("fsdp"))
    return jax.shard_map(
        per_device, mesh=mesh, in_specs=in_specs, out_specs=out_specs, check_vma=False
    )
```

```python
import math

import jax
import jax.numpy as jnp
from jax import lax
from jax.experimental import pallas as pl
from jax.experimental.pallas import tpu as pltpu
from jax.sharding import PartitionSpec as P

WIDTH = 4608
RANK = 256
SLOTS = 3072
LMAX = 64
ROLLS = 48
NP = 16
NZ = 12
NX = 4
FEAT = WIDTH // NP
BLOCK = WIDTH // (NZ * NX)
PER = FEAT // BLOCK
CHUNK = 256
NCH = SLOTS // CHUNK
TILES = 12
HALF = NCH // 2
GROUP = 4
FIRST = 18
FAR_Z = (6, 5, 7, 4, 8, 3, 9, 2, 10, 1, 11)
PIECES = ((0, 48), (48, 32), (80, 32))
NEAR_Z = (3, 9, 2, 10, 1, 11)
FAR_Y = (4, 3, 5, 2, 6, 1, 7)
FAR_P = (8, 7, 9, 6, 10, 5, 11, 4, 12, 3, 13, 2, 14, 1, 15)
kl_coef = 0.1
norm_eps = 1e-06
upper_log = math.log(1.2)
lower_log = math.log(0.8)
F32 = jnp.float32
BF16 = jnp.bfloat16
MESH = pl.DeviceIdType.MESH


def rcopy(src, dst, ssem, rsem, dev):
    return pltpu.make_async_remote_copy(
        src_ref=src, dst_ref=dst, send_sem=ssem, recv_sem=rsem, device_id=dev, device_id_type=MESH
    )


def loop(n, f, start=0):
    def step(i, carry):
        f(i)
        return carry

    lax.fori_loop(start, n, step, jnp.int32(0))


def eye(n, dtype=F32):
    r = lax.broadcasted_iota(jnp.int32, (n, n), 0)
    c = lax.broadcasted_iota(jnp.int32, (n, n), 1)
    return (r == c).astype(F32).astype(dtype)


def contract_last(a, b):
    return lax.dot_general(a, b, (((1,), (1,)), ((), ())), preferred_element_type=F32)


def kernel(
    x_h, gain_h, ad_h, ro_h, drift_h, gap_h, rew_h, grp_h, len_h, dst_h,
    tiles_o,
    xv, rv, adv, gainv, driftv, gapv, rewv, grpv, lenv, dstv,
    rT, zT, dT, W, gfull, gbuf,
    ssp, ssr, ssy, rsv, qp, qr, qy, wv, adv_s, inv_s, len_s,
    WX, CXs, CX, CZs, CM, CN, CD,
    lsem, xsem,
    sAZ, rAZ, sAX, rAX,
    sS, rS, sQ, rQ,
    sCX, rCX, sCM, rCM, sCN, rCN, rCN2, sCD, rCD,
):
    p = lax.axis_index("dp")
    c = lax.axis_index("fsdp")
    z = c // NX
    x = c % NX
    y = p // 2
    core = p % 2
    mine = core * HALF
    theirs = (1 - core) * HALF

    def zdev(z2):
        return (p, z2 * NX + x)

    def xdev(x2):
        return (p, z * NX + x2)

    def ddev(p2):
        return (p2, c)

    def act(x2):
        return lax.rem(x2 + p, 4) != 3

    sibling = (p + 1 - 2 * core, c)
    active = act(x)
    owner = p < TILES
    block = PER * p + jnp.minimum(lax.rem(x + p, 4), PER - 1)
    away = lax.rem(z - block // NX + NZ, NZ)

    small = [
        (ad_h, adv), (gain_h, gainv),
        (ro_h.at[0, pl.ds(theirs * CHUNK, SLOTS // 2)], rv.at[0:SLOTS // 2]),
        (ro_h.at[0, pl.ds(mine * CHUNK, SLOTS // 2)], rv.at[SLOTS // 2:SLOTS]),
        (rew_h, rewv), (grp_h, grpv), (len_h, lenv), (dst_h, dstv),
        (drift_h.at[pl.ds(mine, HALF)], driftv), (gap_h.at[pl.ds(mine, HALF)], gapv),
    ]
    loads = [pltpu.make_async_copy(s, d, lsem.at[i]) for i, (s, d) in enumerate(small)]
    xloads = [
        pltpu.make_async_copy(
            x_h.at[:, pl.ds(pl.multiple_of(first * CHUNK, SLOTS // 2), SLOTS // 2)],
            xv.at[:, i * (SLOTS // 2):(i + 1) * (SLOTS // 2)],
            xsem.at[i],
        )
        for i, first in enumerate((theirs, mine))
    ]
    loads[0].start()
    loads[1].start()
    for d in xloads:
        d.start()
    for d in loads[2:]:
        d.start()

    barrier = pltpu.get_barrier_semaphore()

    def greet(dev):
        pl.semaphore_signal(barrier, inc=1, device_id=dev, device_id_type=MESH)

    for d in FAR_Y:
        for k in range(2):
            greet(ddev(lax.rem(y + d, 8) * 2 + k))
    for d in NEAR_Z:
        greet(zdev(lax.rem(z + d, NZ)))
    for d in (2, 1, 3):
        greet(xdev(lax.rem(x + d, NX)))
    greet(sibling)
    loads[0].wait()
    loads[1].wait()

    @pl.when(active & (away == 0))
    def _():
        row = jnp.concatenate([gainv[...].astype(F32), jnp.ones((1, RANK - BLOCK), F32)], axis=1)
        WX[x, 0:16, :] = jnp.broadcast_to(row, (16, RANK)).astype(BF16)
        WX[x, 16:16 + BLOCK, :] = adv[...]

    pl.semaphore_wait(barrier, len(NEAR_Z) + NX + NP - 2)

    def az(d, s):
        part = WX.at[x, pl.ds(*PIECES[s])]
        return rcopy(part, part, sAZ.at[d, s], rAZ.at[s], zdev(lax.rem(z + d, NZ)))

    def az_all(dirs, s, act_on):
        for d in dirs:
            act_on(az(d, s))

    ROUTES = ((0, NEAR_Z), (3, (3, 2, 1)), (9, (11, 10)))

    @pl.when(active & (away == 0))
    def _():
        for s in range(len(PIECES)):
            az_all((3, 9), s, lambda d: d.start())
        for s in range(len(PIECES)):
            az_all((2, 10, 1, 11), s, lambda d: d.start())

    for d in xloads:
        d.wait()
    for i in range(NCH):
        xt = xv[:, i * CHUNK:(i + 1) * CHUNK].astype(F32)
        ssp[i] = jnp.sum(xt * xt, axis=0, keepdims=True)

    def pair(src, dst, ss, rs, i):
        return rcopy(src, dst, ss.at[i], rs.at[i], sibling)

    def pair_half(part, got, ss, rs):
        return pair(part.at[0:HALF], got, ss, rs, 8)

    def y_send(ys, ss, rs, d):
        return rcopy(ys.at[y], ys.at[y], ss.at[d], rs.at[y], ddev(lax.rem(y + d, 8) * 2 + core))

    def y_start(part, got, ys, ss, rs):
        pair_half(part, got, ss, rs).wait_recv()
        ys[y] = part[HALF:NCH] + got[...]
        for d in FAR_Y:
            y_send(ys, ss, rs, d).start()

    def y_sum(ys, ss, rs):
        for d in range(1, 8):
            y2 = lax.rem(y + d, 8)
            rcopy(ys.at[y2], ys.at[y2], ss.at[d], rs.at[y2], sibling).wait_recv()
        total = ys[0]
        for i in range(1, 8):
            total = total + ys[i]
        return total

    def pair_back(out, ss, rs):
        return pair(out.at[HALF:NCH], out.at[0:HALF], ss, rs, 9)

    pair_half(ssp, ssr, sS, rS).start()

    for d in loads[2:]:
        d.wait()
    ident = eye(RANK, BF16)
    for i in range(NCH):
        rT[i] = contract_last(ident, rv[i * CHUNK:(i + 1) * CHUNK, :]).astype(BF16)

    y_start(ssp, ssr, ssy, sS, rS)

    e48 = eye(ROLLS)

    def col(row):
        return jnp.sum(e48 * row, axis=1, keepdims=True)

    rew = rewv[...]
    grp = grpv[...].astype(F32)
    dst = dstv[...].astype(F32)
    ln = lenv[...].astype(F32)
    rew_c, len_c = col(rew), col(ln)
    same = (col(grp) == grp).astype(F32)
    members = jnp.sum(same, axis=0, keepdims=True)
    mean = jnp.sum(same * rew_c, axis=0, keepdims=True) / members
    var = jnp.sum(same * (rew_c - mean) ** 2, axis=0, keepdims=True) / members
    advantage = (rew - mean) / jnp.sqrt(jnp.maximum(var, 0.25))
    tokens = jnp.sum((col(dst) == dst).astype(F32) * len_c, axis=0, keepdims=True)
    adv_c, inv_c = col(advantage), col(1.0 / tokens)
    slot = lax.broadcasted_iota(jnp.int32, (ROLLS, CHUNK), 1)
    roll = lax.broadcasted_iota(jnp.int32, (ROLLS, CHUNK), 0)
    for i in range(HALF):
        pick = (roll == slot // LMAX + (mine + i) * (CHUNK // LMAX)).astype(F32)
        adv_s[i] = jnp.sum(pick * adv_c, axis=0, keepdims=True)
        inv_s[i] = jnp.sum(pick * inv_c, axis=0, keepdims=True)
        len_s[i] = jnp.sum(pick * len_c, axis=0, keepdims=True)

    def ax(d, s):
        part = WX.at[x, pl.ds(*PIECES[s])]
        return rcopy(part, part, sAX.at[d, s], rAX.at[x, s], xdev(lax.rem(x + d, NX)))

    @pl.when(active)
    def _():
        for s in range(len(PIECES)):
            part = WX.at[x, pl.ds(*PIECES[s])]

            @pl.when(away != 0)
            def _(part=part, s=s):
                rcopy(part, part, rAZ.at[s], rAZ.at[s], sibling).wait_recv()

            for place, dirs in ROUTES[1:]:
                @pl.when(away == place)
                def _(dirs=dirs, s=s):
                    az_all(dirs, s, lambda d: d.start())

            for d in (2, 1, 3):
                ax(d, s).start()

    total = y_sum(ssy, sS, rS)
    rsv[HALF:NCH] = lax.rsqrt(total * (1.0 / WIDTH) + norm_eps)
    pair_back(rsv, sS, rS).start()

    pair_back(rsv, sS, rS).wait_recv()
    for x2 in range(NX):
        @pl.when((x2 != x) & act(x2))
        def _(x2=x2):
            for s, piece in enumerate(PIECES):
                part = WX.at[x2, pl.ds(*piece)]
                rcopy(part, part, rAX.at[x2, s], rAX.at[x2, s], sibling).wait_recv()

    e96 = eye(BLOCK)
    for j in range(PER):
        xs = lax.rem(j + 3 * p, 4)
        W[BLOCK * j:BLOCK * j + BLOCK, :] = WX[xs, 16:16 + BLOCK, :]
        grow = WX[xs, 0:16, :].astype(F32)[0:1, 0:BLOCK]
        gfull[BLOCK * j:BLOCK * j + BLOCK, :] = jnp.broadcast_to(
            jnp.sum(e96 * grow, axis=1, keepdims=True), (BLOCK, CHUNK)
        )

    def qchunk(i):
        h = contract_last(W[...], rv[i * CHUNK:(i + 1) * CHUNK, :])
        xt = xv[:, i * CHUNK:(i + 1) * CHUNK].astype(F32)
        qp[i] = jnp.sum(xt * (h * gfull[...]), axis=0, keepdims=True) * rsv[i]

    for i in range(HALF):
        qchunk(i)
    pair_half(qp, qr, sQ, rQ).start()
    for i in range(HALF, NCH):
        qchunk(i)
    y_start(qp, qr, qy, sQ, rQ)
    for i in range(NCH):
        xt = xv[:, i * CHUNK:(i + 1) * CHUNK].astype(F32)
        zT[i] = (xt * rsv[i] * gfull[...]).astype(BF16)
    shift = y_sum(qy, sQ, rQ)
    drift = driftv[...]
    gap = gapv[...]
    adv_rows = adv_s[...]
    logratio = drift + shift
    ratio = jnp.exp(logratio)
    keep = jnp.where(
        adv_rows >= 0,
        (drift <= jnp.float32(upper_log)).astype(F32),
        (drift >= jnp.float32(lower_log)).astype(F32),
    )
    dshift = inv_s[...] * (-adv_rows * ratio * keep + kl_coef * (1.0 - jnp.exp(gap - logratio)))
    place = lax.rem(lax.broadcasted_iota(jnp.int32, (HALF, 1, CHUNK), 2), LMAX).astype(F32)
    wv[HALF:NCH] = jnp.where(place < len_s[...], dshift, 0.0)
    pair_back(wv, sQ, rQ).start()

    def gsum(chunks):
        total = None
        for i in chunks:
            dT[i] = (rT[i].astype(F32) * wv[i]).astype(BF16)
            term = contract_last(zT[i], dT[i])
            total = term if total is None else total + term
        return total

    gbuf[...] = gsum(range(HALF, NCH))
    pair_back(wv, sQ, rQ).wait_recv()
    g = gsum(range(HALF)) + gbuf[...]
    for j in range(PER):
        for k in range(TILES):
            r0 = BLOCK * j + 16 * (k // 2)
            CXs[j, k] = g[r0:r0 + 16, 128 * (k % 2):128 * (k % 2) + 128].astype(BF16)

    def cx(j, s):
        xs = lax.rem(j + 3 * p, 4)
        part = pl.ds(GROUP * s, GROUP)
        return xs, rcopy(CXs.at[j, part], CX.at[x, part], sCX.at[j, s], rCX.at[x, s], xdev(xs))

    for s in range(TILES // GROUP):
        for j in range(PER):
            xs, d = cx(j, s)

            @pl.when(xs != x)
            def _(d=d):
                d.start()

    for j in range(PER):
        @pl.when(lax.rem(j + 3 * p, 4) == x)
        def _(j=j):
            CX[x] = CXs[j]

    at_home = block // NX == z

    first_lines = block < FIRST

    def near_owner(plane, m):
        return lax.rem(plane // 2 + 7 + m // 2, 8) * 2 + m % 2

    def cn(m):
        return rcopy(CZs.at[pl.ds(2 * m, 2)], CN.at[z], sCN.at[m], rCN.at[z], (near_owner(p, m), block))


    def cm(k):
        return rcopy(CZs.at[k], CM.at[z], sCM.at[k], rCM.at[z], (k, block))

    @pl.when(active)
    def _():
        for s in range(TILES // GROUP):
            part = pl.ds(GROUP * s, GROUP)
            for d in (1, 3, 2):
                x2 = lax.rem(x + d, NX)
                rcopy(CX.at[x2, part], CX.at[x2, part], rCX.at[x2, s], rCX.at[x2, s], sibling).wait_recv()
            total = CX[0, part].astype(F32)
            for i in range(1, NX):
                total = total + CX[i, part].astype(F32)
            CZs[part] = total.astype(BF16)

            @pl.when(first_lines)
            def _(s=s):
                for m in range(GROUP * s // 2, GROUP * s // 2 + GROUP // 2):
                    @pl.when(jnp.logical_not(at_home & (p == near_owner(p, m))))
                    def _(m=m):
                        cn(m).start()

                    @pl.when(at_home & (p == near_owner(p, m)))
                    def _(m=m):
                        CN[z] = CZs[2 * m:2 * m + 2]

            @pl.when(block >= FIRST)
            def _(s=s):
                for k in range(GROUP * s, GROUP * s + GROUP):
                    @pl.when(jnp.logical_not(at_home & (p == k)))
                    def _(k=k):
                        cm(k).start()

                    @pl.when(at_home & (p == k))
                    def _(k=k):
                        CM[z] = CZs[k]

    feeder = c // PER

    def cd(d):
        return rcopy(CD.at[p], CD.at[p], sCD.at[d], rCD.at[p], ddev(lax.rem(p + d, NP)))

    in_first = c < FIRST
    others = c >= FIRST

    def cdn(m, d):
        part = CD.at[pl.ds(2 * m, 2)]
        return rcopy(part, part, sCD.at[d], rCN2.at[m], ddev(lax.rem(p + d, NP)))

    for m in range(6):
        @pl.when(in_first & (p == near_owner(feeder, m)))
        def _(m=m):
            for d in (0,) + FAR_Z[::-1]:
                zz = lax.rem(z + d, NZ)

                def arrive(zz=zz):
                    rcopy(CN.at[zz], CN.at[zz], rCN.at[zz], rCN.at[zz], sibling).wait_recv()

                if d == 0:
                    pl.when(feeder != p)(arrive)
                else:
                    arrive()
            total = CN[0].astype(F32)
            for i in range(1, NZ):
                total = total + CN[i].astype(F32)
            CD[2 * m:2 * m + 2] = total.astype(BF16)
            for d in FAR_P[::-1]:
                cdn(m, d).start()

    for m in range(6):
        @pl.when(in_first & (p != near_owner(feeder, m)))
        def _(m=m):
            part = CD.at[pl.ds(2 * m, 2)]
            rcopy(part, part, rCN2.at[m], rCN2.at[m], sibling).wait_recv()

    @pl.when(owner & others)
    def _():
        for d in (0,) + FAR_Z[::-1]:
            zz = lax.rem(z + d, NZ)

            def arrive(zz=zz):
                rcopy(CM.at[zz], CM.at[zz], rCM.at[zz], rCM.at[zz], sibling).wait_recv()

            if d == 0:
                pl.when(feeder != p)(arrive)
            else:
                arrive()
        tile = CM[0].astype(F32)
        for i in range(1, NZ):
            tile = tile + CM[i].astype(F32)
        CD[p] = tile.astype(BF16)
        for d in FAR_P:
            cd(d).start()

    for k in range(TILES):
        @pl.when((p != k) & others)
        def _(k=k):
            rcopy(CD.at[k], CD.at[k], rCD.at[k], rCD.at[k], sibling).wait_recv()
    tiles_o[...] = CD[...]

    @pl.when(active)
    def _():
        for s in range(len(PIECES)):
            for place, dirs in ROUTES:
                @pl.when(away == place)
                def _(dirs=dirs, s=s):
                    az_all(dirs, s, lambda d: d.wait_send())

            for d in (1, 2, 3):
                ax(d, s).wait_send()
        for k in range(TILES):
            @pl.when((block >= FIRST) & jnp.logical_not(at_home & (p == k)))
            def _(k=k):
                cm(k).wait_send()
        for m in range(6):
            @pl.when(first_lines & jnp.logical_not(at_home & (p == near_owner(p, m))))
            def _(m=m):
                cn(m).wait_send()

    for part, got, ys, out, ss, rs in ((ssp, ssr, ssy, rsv, sS, rS), (qp, qr, qy, wv, sQ, rQ)):
        pair_half(part, got, ss, rs).wait_send()
        for d in range(1, 8):
            y_send(ys, ss, rs, d).wait_send()
        pair_back(out, ss, rs).wait_send()

    for s in range(TILES // GROUP):
        for j in range(PER):
            xs, d = cx(j, s)

            @pl.when(xs != x)
            def _(d=d):
                d.wait_send()

    @pl.when(owner & others)
    def _():
        loop(NP, lambda d: cd(d).wait_send(), 1)

    for m in range(6):
        @pl.when(in_first & (p == near_owner(feeder, m)))
        def _(m=m):
            for d in FAR_P:
                cdn(m, d).wait_send()


def finish(tiles, ad, gain, grad_o, ggain_o):
    for k in range(TILES):
        r0, c0 = 16 * (k // 2), 128 * (k % 2)
        grad_o[r0:r0 + 16, c0:c0 + 128] = tiles[k].astype(F32)
    gsum = jnp.sum(grad_o[...] * ad[...].astype(F32), axis=1, keepdims=True)
    ggain_o[...] = jnp.sum(eye(BLOCK) * gsum, axis=0, keepdims=True) / gain[...].astype(F32)


def per_device(x_slots, gain, adapter, readout, drift, ref_gap, rewards, groups, lengths, dest):
    V = pltpu.VMEM
    D = pltpu.SemaphoreType.DMA
    hbm_spec = pl.BlockSpec(memory_space=pltpu.HBM)
    vmem_spec = pl.BlockSpec(memory_space=pltpu.VMEM)
    chunks = V((NCH, 1, CHUNK), F32)
    half = V((HALF, 1, CHUNK), F32)
    along_y = V((8, HALF, 1, CHUNK), F32)
    tiles = pl.pallas_call(
        kernel,
        out_shape=jax.ShapeDtypeStruct((TILES, 16, 128), BF16),
        in_specs=[hbm_spec] * 10,
        out_specs=vmem_spec,
        scratch_shapes=[
            V((FEAT, SLOTS), BF16), V((SLOTS, RANK), BF16), V((BLOCK, RANK), BF16), V((1, BLOCK), BF16),
            half, half, V((1, ROLLS), F32),
            V((1, ROLLS), jnp.int32), V((1, ROLLS), jnp.int32), V((1, ROLLS), jnp.int32),
            V((NCH, RANK, CHUNK), BF16), V((NCH, FEAT, CHUNK), BF16),
            V((NCH, RANK, CHUNK), BF16), V((FEAT, RANK), BF16), V((FEAT, CHUNK), F32), V((FEAT, RANK), F32),
            chunks, half, along_y, chunks, chunks, half, along_y, chunks, half, half, half,
            V((NX, BLOCK + 16, RANK), BF16),
            V((PER, TILES, 16, 128), BF16), V((NX, TILES, 16, 128), BF16),
            V((TILES, 16, 128), BF16), V((NZ, 16, 128), BF16),
            V((NZ, 2, 16, 128), BF16), V((TILES, 16, 128), BF16),
            D((10,)), D((2,)),
            D((NZ, len(PIECES))), D((len(PIECES),)), D((NX, len(PIECES))), D((NX, len(PIECES))),
            D((10,)), D((10,)), D((10,)), D((10,)),
            D((PER, TILES // GROUP)), D((NX, TILES // GROUP)),
            D((TILES,)), D((NZ,)), D((6,)), D((NZ,)), D((6,)), D((NP,)), D((TILES,)),
        ],
        compiler_params=pltpu.CompilerParams(
            collective_id=0, has_side_effects=True, vmem_limit_bytes=60 * 1024 * 1024
        ),
    )(
        jnp.swapaxes(x_slots[0], 0, 1), gain.reshape(1, BLOCK), adapter, readout,
        drift.reshape(NCH, 1, CHUNK), ref_gap.reshape(NCH, 1, CHUNK), rewards, groups, lengths, dest,
    )
    grad, ggain = pl.pallas_call(
        finish,
        out_shape=(
            jax.ShapeDtypeStruct((BLOCK, RANK), F32),
            jax.ShapeDtypeStruct((1, BLOCK), F32),
        ),
        in_specs=[vmem_spec] * 3,
        out_specs=(vmem_spec, vmem_spec),
    )(tiles, adapter, gain.reshape(1, BLOCK))
    return grad, ggain.reshape(BLOCK)


def solution(mesh):
    in_specs = (
        P("fsdp", None, "dp"),
        P("fsdp"),
        P("fsdp", None),
        P("fsdp", None, None),
        P("fsdp", None),
        P("fsdp", None),
        P("fsdp", None),
        P("fsdp", None),
        P("fsdp", None),
        P("fsdp", None),
    )
    out_specs = (P("fsdp", None), P("fsdp"))
    return jax.shard_map(
        per_device, mesh=mesh, in_specs=in_specs, out_specs=out_specs, check_vma=False
    )
```
